128 devices in a mesh: section: 8 (over z, core), kfac: 16 (over y, x).
Axes of the slice: x: 4, y: 4, z: 4, core: 2. Of those that a mesh axis runs over, the one named last changes fastest.
Arguments:
- top_cotangent: bfloat16 [8, 32, 8192], P(None, None, 'kfac'), may hold values from -6 to 6
- inputs: bfloat16 [8, 8, 32, 8192], P('section'), may hold values from -6 to 6
- proj_weight: bfloat16 [8, 8192, 2048], P('section', None, 'kfac'), may hold values from -0.0625 to 0.0625
- return_weight: bfloat16 [8, 2048, 8192], P('section', 'kfac'), may hold values from -0.125 to 0.125
- owners: int32 [8, 8], P('section'), may hold values from 0 to 15, as said below
- input_inverses: bfloat16 [8, 16, 1024, 1024], P('section', 'kfac'), as said below
- output_inverses: bfloat16 [8, 2, 1024, 1024], P('section'), as said below
Outputs:
- section_cotangents: bfloat16 [8, 8, 32, 8192], P('section', None, None, 'kfac')
- preconditioned: bfloat16 [8, 8192, 2048], P('section', None, 'kfac')
The draws below stay inside these ranges and needn't reach their ends.
Inputs may be any that keep to these rules, and one draw needn't show every extreme that they name: In each section's row no kfac device is named more than once (the eight blocks of a section have eight distinct owners). `input_inverses`: slot o + j of a section holds the inverse for the (j+1)-th block, in block order, that owners assigns to device o; slots that no block uses hold arbitrary values. Each block is symmetric. `output_inverses`: each block is symmetric.
All inputs are finite; a program needn't handle non-finite values.
Results may differ from the reference program's by a relative error of at most 0.035.
Values may be sent and summed in bfloat16 or wider, within the bound.
No kernel may reach another device: no remote copies, remote signals or barrier semaphores. Data moves between devices by JAX's collectives and lax.ppermute only.
A program may use at most 128 MiB of HBM per device.

```python
import math
import jax
import jax.numpy as jnp
from jax import lax

D = 8192
R = 2048
BLK = 1024
CAP = 1
TOK = 32
MICRO = 8
SECTIONS = 8
NB = 8
NG = 2
SLOTS = 16
N_KFAC = 16


def symmetric_blocks(key, count, lowest, highest, mixing):
    diag_key, noise_key = jax.random.split(key)
    diagonal = jnp.exp(jax.random.uniform(diag_key, (count, BLK), jnp.float32, math.log(lowest), math.log(highest)))
    noise = jax.random.normal(noise_key, (count, BLK, BLK), jnp.float32) * mixing
    symmetric = (noise + jnp.swapaxes(noise, 1, 2)) * 0.5
    identity = jnp.eye(BLK, dtype=jnp.float32)
    core = identity + symmetric * (1.0 - identity)
    rooted = jnp.sqrt(diagonal)
    return (core * rooted[:, :, None] * rooted[:, None, :]).astype(jnp.bfloat16)


def draw_owners(key, part):
    key = jax.random.fold_in(key, 7)

    def one_section(section_key):
        first_key, slot_key, order_key = jax.random.split(section_key, 3)
        busiest = jax.random.randint(first_key, (), 0, N_KFAC).astype(jnp.int32)
        shuffled = jax.random.permutation(slot_key, (N_KFAC - 1) * CAP)
        others = (shuffled[:NB - CAP] // CAP).astype(jnp.int32)
        others = others + (others >= busiest).astype(jnp.int32)
        listed = jnp.concatenate([jnp.full((CAP,), busiest, jnp.int32), others])
        return listed[jax.random.permutation(order_key, NB)]
    return jax.vmap(one_section)(jax.random.split(key, SECTIONS))


def draw_input_inverses(key, part):
    key = jax.random.fold_in(key, 11)
    flat = symmetric_blocks(key, SECTIONS * SLOTS, 0.01, 0.1, 0.012)
    return flat.reshape(SECTIONS, SLOTS, BLK, BLK)


def draw_output_inverses(key, part):
    key = jax.random.fold_in(key, 13)
    flat = symmetric_blocks(key, SECTIONS * NG, 0.5, 2.0, 0.012)
    return flat.reshape(SECTIONS, NG, BLK, BLK)


def level_of(stream_key, dims, cuts, least, largest):
    def one(axis_at, parts):
        draws = jax.random.uniform(jax.random.fold_in(jax.random.fold_in(stream_key, 6), axis_at), (parts,), jnp.float32, least / len(cuts), largest / len(cuts))
        return jnp.repeat(jnp.exp(draws), dims[axis_at] // parts).reshape((-1,) + (1,) * (len(dims) - axis_at - 1))

    loudness = one(*cuts[0])
    for cut in cuts[1:]:
        loudness = loudness * one(*cut)
    return loudness


def gaussian(rng, dims, deviation, limit, cuts=(), kind=jnp.bfloat16):
    values = jax.random.normal(rng, dims, jnp.float32) * deviation
    if len(cuts) > 0:
        values = level_of(rng, dims, cuts, -0.22, 0.18) * values
    return jnp.clip(values, min=-limit, max=limit).astype(kind)


def setup_inputs(seed: int = 0) -> dict:
    keys = jax.random.split(jax.random.key(seed), 8)
    return {
        "top_cotangent": gaussian(keys[0], (MICRO, TOK, D), 1.0, 6.0, ((2, 16),)),
        "inputs": gaussian(keys[1], (SECTIONS, MICRO, TOK, D), 1.0, 6.0, ((0, 8),)),
        "proj_weight": gaussian(keys[2], (SECTIONS, D, R), D ** -0.5, 0.0625, ((0, 8), (2, 16))),
        "return_weight": gaussian(keys[3], (SECTIONS, R, D), R ** -0.5, 0.125, ((0, 8), (1, 16))),
        "owners": draw_owners(jax.random.fold_in(keys[7], 71), 0),
        "input_inverses": draw_input_inverses(jax.random.fold_in(keys[7], 71), 0),
        "output_inverses": draw_output_inverses(jax.random.fold_in(keys[7], 71), 0),
    }


def silu_slope(values):
    sigmoid = jax.nn.sigmoid(values)
    return sigmoid * (1.0 + values * (1.0 - sigmoid))


def slot_numbers(owner_row):
    blocks = owner_row.shape[0]
    earlier = jnp.arange(blocks)[None, :] < jnp.arange(blocks)[:, None]
    shared = owner_row[None, :] == owner_row[:, None]
    return jnp.sum(jnp.logical_and(earlier, shared).astype(jnp.int32), axis=1).astype(jnp.int32)


def reference(top_cotangent, inputs, proj_weight, return_weight, owners, input_inverses, output_inverses):
    cotangent = top_cotangent.reshape(MICRO * TOK, D)
    cotangent_list = []
    precond_list = []
    for section_now in range(SECTIONS - 1, -1, -1):
        activations = inputs[section_now].reshape(MICRO * TOK, D)
        weight = proj_weight[section_now]
        hidden = jnp.dot(activations, weight, preferred_element_type=jnp.float32)
        returned = jnp.dot(cotangent, return_weight[section_now].T, preferred_element_type=jnp.float32)
        slope_grad = (returned * silu_slope(hidden)).astype(jnp.bfloat16)
        cotangent = (cotangent.astype(jnp.float32) + jnp.dot(slope_grad, weight.T, preferred_element_type=jnp.float32)).astype(jnp.bfloat16)
        cotangent_list.append(cotangent.reshape(MICRO, TOK, D))
        gradient = jnp.dot(activations.T, slope_grad, preferred_element_type=jnp.float32).astype(jnp.bfloat16)
        owner_row = owners[section_now]
        slot_index = slot_numbers(owner_row)
        block_rows = []
        for block_id in range(NB):
            slot_flat = (owner_row[block_id] * CAP + slot_index[block_id]).astype(jnp.int32)
            factor = lax.dynamic_index_in_dim(input_inverses[section_now], slot_flat, 0, keepdims=False)
            left_product = jnp.dot(factor, gradient[block_id * BLK:(block_id + 1) * BLK], preferred_element_type=jnp.float32).astype(jnp.bfloat16)
            column_parts = [jnp.dot(left_product[:, group_id * BLK:(group_id + 1) * BLK], output_inverses[section_now, group_id], preferred_element_type=jnp.float32) for group_id in range(NG)]
            block_rows.append(jnp.concatenate(column_parts, axis=1).astype(jnp.bfloat16))
        precond_list.append(jnp.concatenate(block_rows, axis=0))
    return jnp.stack(cotangent_list[::-1]), jnp.stack(precond_list[::-1])
```

```python
import jax
import jax.numpy as jnp
from jax import lax
from jax.experimental import pallas as pl
from jax.experimental.pallas import tpu as pltpu
from jax.sharding import PartitionSpec as P

BF = jnp.bfloat16
F32 = jnp.float32
SIDE = 4
AXES = ("section", "kfac")


def silu_slope(values):
    sigmoid = jax.nn.sigmoid(values)
    return sigmoid * (1.0 + values * (1.0 - sigmoid))


def slot_numbers(owner_row):
    blocks = owner_row.shape[0]
    earlier = jnp.arange(blocks)[None, :] < jnp.arange(blocks)[:, None]
    shared = owner_row[None, :] == owner_row[:, None]
    return jnp.sum(jnp.logical_and(earlier, shared).astype(jnp.int32), axis=1)


def shift(block, rows, cols):
    route = []
    for row in range(SIDE):
        for col in range(SIDE):
            source = (row + rows) % SIDE * SIDE + (col + cols) % SIDE
            route.append((source, row * SIDE + col))
    return lax.ppermute(block, "kfac", route)


def shift_section(block, source_section, target_section, rows, cols):
    size = SIDE * SIDE
    route = []
    for row in range(SIDE):
        for col in range(SIDE):
            source = (row + rows) % SIDE * SIDE + (col + cols) % SIDE
            route.append((source_section * size + source, target_section * size + row * SIDE + col))
    return lax.ppermute(block, AXES, route)


def dot_nt(left, right):
    return lax.dot_general(left, right, (((1,), (1,)), ((), ())), preferred_element_type=F32)


def dot_nn(left, right):
    return lax.dot_general(left, right, (((1,), (0,)), ((), ())), preferred_element_type=F32)


def spread_kernel(slots_ref, left_ref, right_ref, out_ref):
    out_ref[...] = jnp.dot(
        left_ref[0], right_ref[...], preferred_element_type=F32
    ).astype(out_ref.dtype)


def spread(slots, left, right, block_count):
    _, height, depth = left.shape
    width = right.shape[1]
    return pl.pallas_call(
        spread_kernel,
        grid_spec=pltpu.PrefetchScalarGridSpec(
            num_scalar_prefetch=1,
            grid=(block_count,),
            in_specs=[
                pl.BlockSpec((1, height, depth), lambda b, slots: (slots[b], 0, 0)),
                pl.BlockSpec((depth, width), lambda b, slots: (0, 0)),
            ],
            out_specs=pl.BlockSpec((height, width), lambda b, slots: (b, 0)),
        ),
        out_shape=jax.ShapeDtypeStruct((block_count * height, width), BF),
        compiler_params=pltpu.CompilerParams(vmem_limit_bytes=16 * 1024 * 1024),
        cost_estimate=pl.CostEstimate(
            flops=2 * block_count * height * depth * width,
            bytes_accessed=2 * block_count * height * (depth + width),
            transcendentals=0,
        ),
    )(slots, left, right)


def on_device(
    top_cotangent, inputs, proj_weight, return_weight, owners, input_inverses, output_inverses
):
    section_count = lax.axis_size("section")
    section_here = lax.axis_index("section")
    kfac_here = lax.axis_index("kfac")
    row, col = kfac_here // SIDE, kfac_here % SIDE
    micro, per_micro, shard_width = top_cotangent.shape
    tokens = micro * per_micro
    x = inputs[0].reshape(tokens, -1)
    weight = proj_weight[0]
    returning = return_weight[0]
    width, stripe = weight.shape
    quarter = width // SIDE
    block_width = input_inverses.shape[2]
    block_count = width // block_width
    group_count = output_inverses.shape[1]

    back_parts = [lax.dynamic_slice(returning, (0, row * quarter), (stripe, quarter))]
    proj_parts = [lax.dynamic_slice(weight, (row * quarter, 0), (quarter, stripe))]
    for rows in range(1, SIDE):
        there = (row - rows) % SIDE
        back_parts.append(
            shift(lax.dynamic_slice(returning, (0, there * quarter), (stripe, quarter)), rows, 0)
        )
    top = top_cotangent.reshape(tokens, shard_width)
    incoming = [top] + [shift(top, 0, cols) for cols in range(1, SIDE)]
    for rows in range(1, SIDE):
        there = (row - rows) % SIDE
        proj_parts.append(
            shift(lax.dynamic_slice(weight, (there * quarter, 0), (quarter, stripe)), rows, 0)
        )
    slopes_here = silu_slope(dot_nn(x, weight))
    slope_parts = [slopes_here] + [shift(slopes_here, rows, 0) for rows in range(1, SIDE)]

    place = [(row + rows) % SIDE * stripe for rows in range(SIDE)]
    block = SIDE * stripe
    back_weight = jnp.zeros((block, quarter), BF)
    proj_block = jnp.zeros((quarter, block), BF)
    factor = jnp.zeros((tokens, block), F32)
    for rows in range(SIDE):
        back_weight = lax.dynamic_update_slice(back_weight, back_parts[rows], (place[rows], 0))
        proj_block = lax.dynamic_update_slice(proj_block, proj_parts[rows], (0, place[rows]))
        factor = lax.dynamic_update_slice(factor, slope_parts[rows], (0, place[rows]))
    back_rel = [
        lax.dynamic_slice(back_weight, (0, (col + cols) % SIDE * shard_width), (block, shard_width))
        for cols in range(SIDE)
    ]
    proj_rel = [
        lax.dynamic_slice(proj_block, ((col - cols) % SIDE * shard_width, 0), (shard_width, block))
        for cols in range(SIDE)
    ]

    targets = owners[0] + slot_numbers(owners[0])
    mine = targets == kfac_here
    block_here = jnp.sum(jnp.where(mine, jnp.arange(block_count, dtype=jnp.int32), 0))
    x_block = lax.dynamic_slice(x, (0, block_here * block_width), (tokens, block_width))
    left_here = dot_nt(input_inverses[0, 0], x_block).astype(BF)
    left_all = lax.all_gather(left_here, "kfac", axis=0)

    group_here = kfac_here * stripe // block_width
    per_group = SIDE // group_count
    out_cols = lax.dynamic_slice(
        output_inverses[0],
        (group_here, 0, kfac_here * stripe % block_width),
        (1, block_width, stripe),
    ).reshape(per_group, SIDE, stripe, stripe)
    out_rel = [
        lax.dynamic_index_in_dim(out_cols, (col + cols) % SIDE, 1, keepdims=False).reshape(
            per_group * stripe, stripe
        )
        for cols in range(SIDE)
    ]

    outputs = jnp.zeros((tokens, shard_width), BF)
    slope_saved = jnp.zeros((tokens, per_group * stripe), BF)
    for section in range(section_count - 1, -1, -1):
        active = section_here == section
        back = sum(dot_nt(c, u) for c, u in zip(incoming, back_rel))
        back_sent = back.astype(BF)
        for rows in range(1, SIDE):
            back = back + shift_section(back_sent, section, section, rows, 0).astype(F32)
        slope = (back * factor).astype(BF)
        slope_group = lax.dynamic_slice(
            slope, (0, group_here * per_group * stripe), (tokens, per_group * stripe)
        )
        slope_saved = jnp.where(active, slope_group, slope_saved)
        summed = incoming[0].astype(F32) + dot_nt(slope, proj_rel[0])
        for cols in range(1, SIDE):
            part = dot_nt(slope, proj_rel[cols]).astype(BF)
            summed = summed + shift_section(part, section, section, 0, cols).astype(F32)
        updated = summed.astype(BF)
        outputs = jnp.where(active, updated, outputs)
        if section > 0:
            incoming = [
                shift_section(updated, section, section - 1, 0, cols) for cols in range(SIDE)
            ]

    right = dot_nn(slope_saved, out_rel[0])
    for cols in range(1, SIDE):
        right = right + dot_nn(shift(slope_saved, 0, cols), out_rel[cols])
    result = spread(targets, left_all, right.astype(BF), block_count)
    return outputs.reshape(1, micro, per_micro, shard_width), result[None]


def solution(mesh):
    return jax.shard_map(
        on_device,
        mesh=mesh,
        in_specs=(
            P(None, None, "kfac"),
            P("section", None, None, None),
            P("section", None, "kfac"),
            P("section", "kfac", None),
            P("section", None),
            P("section", "kfac", None, None),
            P("section", None, None, None),
        ),
        out_specs=(P("section", None, None, "kfac"), P("section", None, "kfac")),
        check_vma=False,
    )
```

```python
import jax
import jax.numpy as jnp
from jax import lax
from jax.experimental import pallas as pl
from jax.experimental.pallas import tpu as pltpu
from jax.sharding import PartitionSpec as P

BF = jnp.bfloat16
F32 = jnp.float32
SIDE = 4
AXES = ("section", "kfac")


def silu_slope(values):
    sigmoid = jax.nn.sigmoid(values)
    return sigmoid * (1.0 + values * (1.0 - sigmoid))


def slot_numbers(owner_row):
    blocks = owner_row.shape[0]
    earlier = jnp.arange(blocks)[None, :] < jnp.arange(blocks)[:, None]
    shared = owner_row[None, :] == owner_row[:, None]
    return jnp.sum(jnp.logical_and(earlier, shared).astype(jnp.int32), axis=1)


def shift(block, rows, cols):
    route = []
    for row in range(SIDE):
        for col in range(SIDE):
            source = (row + rows) % SIDE * SIDE + (col + cols) % SIDE
            route.append((source, row * SIDE + col))
    return lax.ppermute(block, "kfac", route)


def shift_core(block, sections, step, rows, cols):
    size = SIDE * SIDE
    route = []
    for section in sections:
        for row in range(SIDE):
            for col in range(SIDE):
                source = (row + rows) % SIDE * SIDE + (col + cols) % SIDE
                route.append((section * size + source, (section - step) * size + row * SIDE + col))
    return lax.ppermute(block, AXES, route)


def dot_nt(left, right):
    return lax.dot_general(left, right, (((1,), (1,)), ((), ())), preferred_element_type=F32)


def dot_nn(left, right):
    return lax.dot_general(left, right, (((1,), (0,)), ((), ())), preferred_element_type=F32)


def move(position, sources, out_shapes, moves):
    count = len(sources)

    def body(position_ref, *refs):
        sems = refs[-1]
        pairs = moves(position_ref[0], position_ref[1], refs[:count], refs[count:-1])
        copies = [
            pltpu.make_async_copy(source, target, sems.at[i])
            for i, (source, target) in enumerate(pairs)
        ]
        for copy in copies:
            copy.start()
        for copy in copies:
            copy.wait()

    return pl.pallas_call(
        body,
        in_specs=[pl.BlockSpec(memory_space=pltpu.SMEM)] + [pl.BlockSpec(memory_space=pl.ANY)] * count,
        out_specs=[pl.BlockSpec(memory_space=pl.ANY)] * len(out_shapes),
        out_shape=out_shapes,
        scratch_shapes=[pltpu.SemaphoreType.DMA((SIDE * SIDE,))],
        cost_estimate=pl.CostEstimate(
            flops=0,
            bytes_accessed=2 * sum(o.size * o.dtype.itemsize for o in out_shapes),
            transcendentals=0,
        ),
    )(position, *sources)


def chunk(index, size):
    return pl.ds(pl.multiple_of(lax.rem(index + SIDE, SIDE) * size, size), size)


def whole(count):
    return [pl.BlockSpec(memory_space=pltpu.VMEM)] * count


def back_kernel(*refs):
    shards, weight_ref, out_ref = refs[:SIDE], refs[SIDE], refs[SIDE + 1]
    width = shards[0].shape[1]
    total = dot_nt(shards[0][...], weight_ref[:, :width])
    for j in range(1, SIDE):
        total = total + dot_nt(shards[j][...], weight_ref[:, j * width : (j + 1) * width])
    out_ref[...] = total.astype(out_ref.dtype)


def back_product(shards, weight):
    tokens, width = shards[0].shape
    block = weight.shape[0]
    return pl.pallas_call(
        back_kernel,
        in_specs=whole(SIDE + 1),
        out_specs=pl.BlockSpec(memory_space=pltpu.VMEM),
        out_shape=jax.ShapeDtypeStruct((tokens, block), BF),
        cost_estimate=pl.CostEstimate(
            flops=2 * tokens * width * SIDE * block,
            bytes_accessed=2 * SIDE * width * (tokens + block) + 2 * tokens * block,
            transcendentals=0,
        ),
    )(*shards, weight)


def proj_kernel(*refs):
    parts, factor_ref, weight_ref = refs[:SIDE], refs[SIDE], refs[SIDE + 1]
    slope_ref, own_ref, sent = refs[SIDE + 2], refs[SIDE + 3], refs[SIDE + 4 :]
    back = parts[0][...].astype(F32)
    for j in range(1, SIDE):
        back = back + parts[j][...].astype(F32)
    slope = (back * factor_ref[...]).astype(BF)
    slope_ref[...] = slope
    width = own_ref.shape[1]
    for j in range(1, SIDE):
        product = dot_nt(slope, weight_ref[j * width : (j + 1) * width, :])
        sent[j - 1][...] = product.astype(BF)
    own_ref[...] = dot_nt(slope, weight_ref[:width, :])


def proj_product(parts, factor, weight):
    tokens, block = factor.shape
    width = weight.shape[0] // SIDE
    bf = jax.ShapeDtypeStruct((tokens, width), BF)
    return pl.pallas_call(
        proj_kernel,
        in_specs=whole(SIDE + 2),
        out_specs=whole(SIDE + 1),
        out_shape=[
            jax.ShapeDtypeStruct((tokens, block), BF),
            jax.ShapeDtypeStruct((tokens, width), F32),
        ]
        + [bf] * (SIDE - 1),
        cost_estimate=pl.CostEstimate(
            flops=2 * tokens * width * SIDE * block,
            bytes_accessed=2 * SIDE * width * (tokens + block) + 12 * tokens * block,
            transcendentals=0,
        ),
    )(*parts, factor, weight)


def left_kernel(block_ref, factor_ref, x_ref, out_ref):
    out_ref[...] = dot_nt(factor_ref[...], x_ref[...]).astype(out_ref.dtype)


def left_product(block_here, factor, x):
    size = factor.shape[0]
    tokens = x.shape[0]
    return pl.pallas_call(
        left_kernel,
        grid_spec=pltpu.PrefetchScalarGridSpec(
            num_scalar_prefetch=1,
            grid=(1,),
            in_specs=[
                pl.BlockSpec((size, size), lambda i, block: (0, 0)),
                pl.BlockSpec((tokens, size), lambda i, block: (0, block[0])),
            ],
            out_specs=pl.BlockSpec((size, tokens), lambda i, block: (0, 0)),
        ),
        out_shape=jax.ShapeDtypeStruct((size, tokens), BF),
        cost_estimate=pl.CostEstimate(
            flops=2 * size * size * tokens,
            bytes_accessed=2 * size * (size + 2 * tokens),
            transcendentals=0,
        ),
    )(block_here, factor, x)


def spread_kernel(slots_ref, left_ref, right_ref, out_ref):
    out_ref[...] = dot_nn(left_ref[...], right_ref[...]).astype(out_ref.dtype)


def spread(slots, left, right, height):
    depth = left.shape[1]
    width = right.shape[1]
    block_count = slots.shape[0]
    return pl.pallas_call(
        spread_kernel,
        grid_spec=pltpu.PrefetchScalarGridSpec(
            num_scalar_prefetch=1,
            grid=(block_count,),
            in_specs=[
                pl.BlockSpec((height, depth), lambda b, slots: (slots[b], 0)),
                pl.BlockSpec((depth, width), lambda b, slots: (0, 0)),
            ],
            out_specs=pl.BlockSpec((height, width), lambda b, slots: (b, 0)),
        ),
        out_shape=jax.ShapeDtypeStruct((block_count * height, width), BF),
        cost_estimate=pl.CostEstimate(
            flops=2 * block_count * height * depth * width,
            bytes_accessed=2 * block_count * height * (depth + width),
            transcendentals=0,
        ),
    )(slots, left, right)


def on_device(
    top_cotangent, inputs, proj_weight, return_weight, owners, input_inverses, output_inverses
):
    section_count = lax.axis_size("section")
    section_here = lax.axis_index("section")
    kfac_here = lax.axis_index("kfac")
    row, col = kfac_here // SIDE, kfac_here % SIDE
    micro, per_micro, shard_width = top_cotangent.shape
    tokens = micro * per_micro
    x = inputs[0].reshape(tokens, -1)
    weight = proj_weight[0]
    returning = return_weight[0]
    width, stripe = weight.shape
    quarter = width // SIDE
    block_width = input_inverses.shape[2]
    block_count = width // block_width
    group_count = output_inverses.shape[1]

    position = jnp.stack([row, col]).astype(jnp.int32)
    block = SIDE * stripe
    back_cut = move(
        position,
        [returning],
        [jax.ShapeDtypeStruct((stripe, quarter), BF)] * SIDE,
        lambda r, c, ins, outs: [
            (ins[0].at[:, chunk(r - j, quarter)], outs[j]) for j in range(SIDE)
        ],
    )
    proj_cut = move(
        position,
        [weight],
        [jax.ShapeDtypeStruct((quarter, stripe), BF)] * SIDE,
        lambda r, c, ins, outs: [
            (ins[0].at[chunk(r - j, quarter), :], outs[j]) for j in range(SIDE)
        ],
    )
    back_parts = [back_cut[0]] + [shift(back_cut[j], j, 0) for j in range(1, SIDE)]
    top = top_cotangent.reshape(tokens, shard_width)
    first = list(range(section_count - 1, 0, -2))
    second = list(range(section_count - 2, -1, -2))
    incoming = [top] + [shift_core(top, first, 0, 0, j) for j in range(1, SIDE)]
    slopes_here = silu_slope(dot_nn(x, weight))
    slope_parts = [slopes_here] + [shift(slopes_here, j, 0) for j in range(1, SIDE)]
    proj_parts = [proj_cut[0]] + [shift(proj_cut[j], j, 0) for j in range(1, SIDE)]
    (back_weight,) = move(
        position,
        back_parts,
        [jax.ShapeDtypeStruct((block, quarter), BF)],
        lambda r, c, ins, outs: [
            (
                ins[j].at[:, chunk(c + k, shard_width)],
                outs[0].at[chunk(r + j, stripe), pl.ds(k * shard_width, shard_width)],
            )
            for j in range(SIDE)
            for k in range(SIDE)
        ],
    )
    (proj_block,) = move(
        position,
        proj_parts,
        [jax.ShapeDtypeStruct((quarter, block), BF)],
        lambda r, c, ins, outs: [
            (
                ins[j].at[chunk(c - k, shard_width), :],
                outs[0].at[pl.ds(k * shard_width, shard_width), chunk(r + j, stripe)],
            )
            for j in range(SIDE)
            for k in range(SIDE)
        ],
    )
    (factor,) = move(
        position,
        slope_parts,
        [jax.ShapeDtypeStruct((tokens, block), F32)],
        lambda r, c, ins, outs: [
            (ins[j], outs[0].at[:, chunk(r + j, stripe)]) for j in range(SIDE)
        ],
    )

    targets = owners[0] + slot_numbers(owners[0])
    mine = targets == kfac_here
    block_here = jnp.sum(jnp.where(mine, jnp.arange(block_count, dtype=jnp.int32), 0))
    left_here = left_product(block_here[None], input_inverses[0, 0], x)
    left_all = lax.all_gather(left_here, "kfac", axis=0, tiled=True)

    group_here = kfac_here * stripe // block_width
    per_group = SIDE // group_count
    out_cols = lax.dynamic_slice(
        output_inverses[0],
        (group_here, 0, kfac_here * stripe % block_width),
        (1, block_width, stripe),
    ).reshape(per_group, SIDE, stripe, stripe)
    out_rel = [
        lax.dynamic_index_in_dim(out_cols, (col + cols) % SIDE, 1, keepdims=False).reshape(
            per_group * stripe, stripe
        )
        for cols in range(SIDE)
    ]

    outputs = jnp.zeros((tokens, shard_width), BF)
    slope_saved = jnp.zeros((tokens, per_group * stripe), BF)
    for section in range(section_count - 1, -1, -1):
        active = section_here == section
        here = first if section in first else second
        back = back_product(incoming, back_weight)
        parts = [back] + [shift_core(back, here, 0, j, 0) for j in range(1, SIDE)]
        slope, own, *sent = proj_product(parts, factor, proj_block)
        slope_group = lax.dynamic_slice(
            slope, (0, group_here * per_group * stripe), (tokens, per_group * stripe)
        )
        slope_saved = jnp.where(active, slope_group, slope_saved)
        summed = incoming[0].astype(F32) + own
        for j in range(1, SIDE):
            summed = summed + shift_core(sent[j - 1], here, 0, 0, j).astype(F32)
        updated = summed.astype(BF)
        outputs = jnp.where(active, updated, outputs)
        if section > 0:
            senders = [s for s in here if s > 0]
            incoming = [shift_core(updated, senders, 1, 0, j) for j in range(SIDE)]

    right = dot_nn(slope_saved, out_rel[0])
    for cols in range(1, SIDE):
        right = right + dot_nn(shift(slope_saved, 0, cols), out_rel[cols])
    result = spread(targets, left_all, right.astype(BF), block_width)
    return outputs.reshape(1, micro, per_micro, shard_width), result[None]


def solution(mesh):
    return jax.shard_map(
        on_device,
        mesh=mesh,
        in_specs=(
            P(None, None, "kfac"),
            P("section", None, None, None),
            P("section", None, "kfac"),
            P("section", "kfac", None),
            P("section", None),
            P("section", "kfac", None, None),
            P("section", None, None, None),
        ),
        out_specs=(P("section", None, None, "kfac"), P("section", None, "kfac")),
        check_vma=False,
    )
```

```python
import jax
import jax.numpy as jnp
from jax import lax
from jax.experimental import pallas as pl
from jax.experimental.pallas import tpu as pltpu
from jax.sharding import PartitionSpec as P

BF = jnp.bfloat16
F32 = jnp.float32
SIDE = 4
AXES = ("section", "kfac")


def silu_slope(values):
    sigmoid = jax.nn.sigmoid(values)
    return sigmoid * (1.0 + values * (1.0 - sigmoid))


def slot_numbers(owner_row):
    blocks = owner_row.shape[0]
    earlier = jnp.arange(blocks)[None, :] < jnp.arange(blocks)[:, None]
    shared = owner_row[None, :] == owner_row[:, None]
    return jnp.sum(jnp.logical_and(earlier, shared).astype(jnp.int32), axis=1)


def shift(block, rows, cols):
    route = []
    for row in range(SIDE):
        for col in range(SIDE):
            source = (row + rows) % SIDE * SIDE + (col + cols) % SIDE
            route.append((source, row * SIDE + col))
    return lax.ppermute(block, "kfac", route)


def shift_core(block, sections, step, rows, cols):
    size = SIDE * SIDE
    route = []
    for section in sections:
        for row in range(SIDE):
            for col in range(SIDE):
                source = (row + rows) % SIDE * SIDE + (col + cols) % SIDE
                route.append((section * size + source, (section - step) * size + row * SIDE + col))
    return lax.ppermute(block, AXES, route)


def dot_nt(left, right):
    return lax.dot_general(left, right, (((1,), (1,)), ((), ())), preferred_element_type=F32)


def dot_nn(left, right):
    return lax.dot_general(left, right, (((1,), (0,)), ((), ())), preferred_element_type=F32)


def move(position, sources, out_shapes, moves):
    count = len(sources)

    def body(position_ref, *refs):
        for source, target in moves(position_ref[0], position_ref[1], refs[:count], refs[count:]):
            target[...] = source[...]

    return pl.pallas_call(
        body,
        in_specs=[pl.BlockSpec(memory_space=pltpu.SMEM)] + whole(count),
        out_specs=whole(len(out_shapes)),
        out_shape=out_shapes,
        cost_estimate=pl.CostEstimate(
            flops=0,
            bytes_accessed=2 * sum(o.size * o.dtype.itemsize for o in out_shapes),
            transcendentals=0,
        ),
    )(position, *sources)


def chunk(index, size):
    return pl.ds(pl.multiple_of(lax.rem(index + SIDE, SIDE) * size, size), size)


def whole(count):
    return [pl.BlockSpec(memory_space=pltpu.VMEM)] * count


def back_kernel(*refs):
    shards, weight_ref, out_ref = refs[:SIDE], refs[SIDE], refs[SIDE + 1]
    width = shards[0].shape[1]
    total = dot_nt(shards[0][...], weight_ref[:, :width])
    for j in range(1, SIDE):
        total = total + dot_nt(shards[j][...], weight_ref[:, j * width : (j + 1) * width])
    out_ref[...] = total.astype(out_ref.dtype)


def back_product(shards, weight):
    tokens, width = shards[0].shape
    block = weight.shape[0]
    return pl.pallas_call(
        back_kernel,
        in_specs=whole(SIDE + 1),
        out_specs=pl.BlockSpec(memory_space=pltpu.VMEM),
        out_shape=jax.ShapeDtypeStruct((tokens, block), BF),
        cost_estimate=pl.CostEstimate(
            flops=2 * tokens * width * SIDE * block,
            bytes_accessed=2 * SIDE * width * (tokens + block) + 2 * tokens * block,
            transcendentals=0,
        ),
    )(*shards, weight)


def proj_kernel(*refs):
    parts, factor_ref, weight_ref = refs[:SIDE], refs[SIDE], refs[SIDE + 1]
    slope_ref, own_ref, sent = refs[SIDE + 2], refs[SIDE + 3], refs[SIDE + 4 :]
    back = parts[0][...].astype(F32)
    for j in range(1, SIDE):
        back = back + parts[j][...].astype(F32)
    slope = (back * factor_ref[...]).astype(BF)
    slope_ref[...] = slope
    width = own_ref.shape[1]
    for j in range(1, SIDE):
        product = dot_nt(slope, weight_ref[j * width : (j + 1) * width, :])
        sent[j - 1][...] = product.astype(BF)
    own_ref[...] = dot_nt(slope, weight_ref[:width, :])


def proj_product(parts, factor, weight):
    tokens, block = factor.shape
    width = weight.shape[0] // SIDE
    bf = jax.ShapeDtypeStruct((tokens, width), BF)
    return pl.pallas_call(
        proj_kernel,
        in_specs=whole(SIDE + 2),
        out_specs=whole(SIDE + 1),
        out_shape=[
            jax.ShapeDtypeStruct((tokens, block), BF),
            jax.ShapeDtypeStruct((tokens, width), F32),
        ]
        + [bf] * (SIDE - 1),
        cost_estimate=pl.CostEstimate(
            flops=2 * tokens * width * SIDE * block,
            bytes_accessed=2 * SIDE * width * (tokens + block) + 12 * tokens * block,
            transcendentals=0,
        ),
    )(*parts, factor, weight)


def left_kernel(block_ref, factor_ref, x_ref, out_ref):
    out_ref[...] = dot_nt(factor_ref[...], x_ref[...]).astype(out_ref.dtype)


def left_product(block_here, factor, x):
    size = factor.shape[0]
    tokens = x.shape[0]
    return pl.pallas_call(
        left_kernel,
        grid_spec=pltpu.PrefetchScalarGridSpec(
            num_scalar_prefetch=1,
            grid=(1,),
            in_specs=[
                pl.BlockSpec((size, size), lambda i, block: (0, 0)),
                pl.BlockSpec((tokens, size), lambda i, block: (0, block[0])),
            ],
            out_specs=pl.BlockSpec((size, tokens), lambda i, block: (0, 0)),
        ),
        out_shape=jax.ShapeDtypeStruct((size, tokens), BF),
        cost_estimate=pl.CostEstimate(
            flops=2 * size * size * tokens,
            bytes_accessed=2 * size * (size + 2 * tokens),
            transcendentals=0,
        ),
    )(block_here, factor, x)


def spread_kernel(slots_ref, left_ref, right_ref, out_ref):
    out_ref[...] = dot_nn(left_ref[...], right_ref[...]).astype(out_ref.dtype)


def spread(slots, left, right, height):
    depth = left.shape[1]
    width = right.shape[1]
    block_count = slots.shape[0]
    return pl.pallas_call(
        spread_kernel,
        grid_spec=pltpu.PrefetchScalarGridSpec(
            num_scalar_prefetch=1,
            grid=(block_count,),
            in_specs=[
                pl.BlockSpec((height, depth), lambda b, slots: (slots[b], 0)),
                pl.BlockSpec((depth, width), lambda b, slots: (0, 0)),
            ],
            out_specs=pl.BlockSpec((height, width), lambda b, slots: (b, 0)),
        ),
        out_shape=jax.ShapeDtypeStruct((block_count * height, width), BF),
        cost_estimate=pl.CostEstimate(
            flops=2 * block_count * height * depth * width,
            bytes_accessed=2 * block_count * height * (depth + width),
            transcendentals=0,
        ),
    )(slots, left, right)


def on_device(
    top_cotangent, inputs, proj_weight, return_weight, owners, input_inverses, output_inverses
):
    section_count = lax.axis_size("section")
    section_here = lax.axis_index("section")
    kfac_here = lax.axis_index("kfac")
    row, col = kfac_here // SIDE, kfac_here % SIDE
    micro, per_micro, shard_width = top_cotangent.shape
    tokens = micro * per_micro
    x = inputs[0].reshape(tokens, -1)
    weight = proj_weight[0]
    returning = return_weight[0]
    width, stripe = weight.shape
    quarter = width // SIDE
    block_width = input_inverses.shape[2]
    block_count = width // block_width
    group_count = output_inverses.shape[1]

    position = jnp.stack([row, col]).astype(jnp.int32)
    block = SIDE * stripe
    back_cut = move(
        position,
        [returning],
        [jax.ShapeDtypeStruct((stripe, quarter), BF)] * SIDE,
        lambda r, c, ins, outs: [
            (ins[0].at[:, chunk(r - j, quarter)], outs[j]) for j in range(SIDE)
        ],
    )
    proj_cut = move(
        position,
        [weight],
        [jax.ShapeDtypeStruct((quarter, stripe), BF)] * SIDE,
        lambda r, c, ins, outs: [
            (ins[0].at[chunk(r - j, quarter), :], outs[j]) for j in range(SIDE)
        ],
    )
    back_parts = [back_cut[0]] + [shift(back_cut[j], j, 0) for j in range(1, SIDE)]
    top = top_cotangent.reshape(tokens, shard_width)
    first = list(range(section_count - 1, 0, -2))
    second = list(range(section_count - 2, -1, -2))
    incoming = [top] + [shift_core(top, first, 0, 0, j) for j in range(1, SIDE)]
    slopes_here = silu_slope(dot_nn(x, weight))
    slope_parts = [slopes_here] + [shift(slopes_here, j, 0) for j in range(1, SIDE)]
    proj_parts = [proj_cut[0]] + [shift(proj_cut[j], j, 0) for j in range(1, SIDE)]
    (back_weight,) = move(
        position,
        back_parts,
        [jax.ShapeDtypeStruct((block, quarter), BF)],
        lambda r, c, ins, outs: [
            (
                ins[j].at[:, chunk(c + k, shard_width)],
                outs[0].at[chunk(r + j, stripe), pl.ds(k * shard_width, shard_width)],
            )
            for j in range(SIDE)
            for k in range(SIDE)
        ],
    )
    (proj_block,) = move(
        position,
        proj_parts,
        [jax.ShapeDtypeStruct((quarter, block), BF)],
        lambda r, c, ins, outs: [
            (
                ins[j].at[chunk(c - k, shard_width), :],
                outs[0].at[pl.ds(k * shard_width, shard_width), chunk(r + j, stripe)],
            )
            for j in range(SIDE)
            for k in range(SIDE)
        ],
    )
    (factor,) = move(
        position,
        slope_parts,
        [jax.ShapeDtypeStruct((tokens, block), F32)],
        lambda r, c, ins, outs: [
            (ins[j], outs[0].at[:, chunk(r + j, stripe)]) for j in range(SIDE)
        ],
    )

    targets = owners[0] + slot_numbers(owners[0])
    mine = targets == kfac_here
    block_here = jnp.sum(jnp.where(mine, jnp.arange(block_count, dtype=jnp.int32), 0))
    left_here = left_product(block_here[None], input_inverses[0, 0], x)
    left_all = lax.all_gather(left_here, "kfac", axis=0, tiled=True)

    group_here = kfac_here * stripe // block_width
    per_group = SIDE // group_count
    out_cols = lax.dynamic_slice(
        output_inverses[0],
        (group_here, 0, kfac_here * stripe % block_width),
        (1, block_width, stripe),
    ).reshape(per_group, SIDE, stripe, stripe)
    out_rel = [
        lax.dynamic_index_in_dim(out_cols, (col + cols) % SIDE, 1, keepdims=False).reshape(
            per_group * stripe, stripe
        )
        for cols in range(SIDE)
    ]

    outputs = jnp.zeros((tokens, shard_width), BF)
    slope_saved = jnp.zeros((tokens, per_group * stripe), BF)
    for section in range(section_count - 1, -1, -1):
        active = section_here == section
        here = first if section in first else second
        back = back_product(incoming, back_weight)
        parts = [back] + [shift_core(back, here, 0, j, 0) for j in range(1, SIDE)]
        slope, own, *sent = proj_product(parts, factor, proj_block)
        slope_group = lax.dynamic_slice(
            slope, (0, group_here * per_group * stripe), (tokens, per_group * stripe)
        )
        slope_saved = jnp.where(active, slope_group, slope_saved)
        summed = incoming[0].astype(F32) + own
        for j in range(1, SIDE):
            summed = summed + shift_core(sent[j - 1], here, 0, 0, j).astype(F32)
        updated = summed.astype(BF)
        outputs = jnp.where(active, updated, outputs)
        if section > 0:
            senders = [s for s in here if s > 0]
            incoming = [shift_core(updated, senders, 1, 0, j) for j in range(SIDE)]

    right = dot_nn(slope_saved, out_rel[0])
    for cols in range(1, SIDE):
        right = right + dot_nn(shift(slope_saved, 0, cols), out_rel[cols])
    result = spread(targets, left_all, right.astype(BF), block_width)
    return outputs.reshape(1, micro, per_micro, shard_width), result[None]


def solution(mesh):
    return jax.shard_map(
        on_device,
        mesh=mesh,
        in_specs=(
            P(None, None, "kfac"),
            P("section", None, None, None),
            P("section", None, "kfac"),
            P("section", "kfac", None),
            P("section", None),
            P("section", "kfac", None, None),
            P("section", None, None, None),
        ),
        out_specs=(P("section", None, None, "kfac"), P("section", None, "kfac")),
        check_vma=False,
    )
```

```python
import jax
import jax.numpy as jnp
from jax import lax
from jax.experimental import pallas as pl
from jax.experimental.pallas import tpu as pltpu
from jax.sharding import PartitionSpec as P

BF = jnp.bfloat16
F32 = jnp.float32
SIDE = 4


def silu_slope(values):
    sigmoid = jax.nn.sigmoid(values)
    return sigmoid * (1.0 + values * (1.0 - sigmoid))


def slot_numbers(owner_row):
    blocks = owner_row.shape[0]
    earlier = jnp.arange(blocks)[None, :] < jnp.arange(blocks)[:, None]
    shared = owner_row[None, :] == owner_row[:, None]
    return jnp.sum(jnp.logical_and(earlier, shared).astype(jnp.int32), axis=1)


def permute_grid(block, source):
    route = []
    for row in range(SIDE):
        for col in range(SIDE):
            from_row, from_col = source(row, col)
            route.append((from_row * SIDE + from_col, row * SIDE + col))
    return lax.ppermute(block, "kfac", route)


def from_col(block, distance):
    return permute_grid(block, lambda row, col: (row, (col + distance) % SIDE))


def swap_cores(block):
    sections = lax.axis_size("section")
    return lax.ppermute(block, "section", [(i, i ^ 1) for i in range(sections)])


def pass_down(block):
    sections = lax.axis_size("section")
    return lax.ppermute(block, "section", [(i, i - 2) for i in range(2, sections)])


def sum_rows(block):
    near = permute_grid(block, lambda row, col: (row ^ 1, col))
    half = (block.astype(F32) + near.astype(F32)).astype(BF)
    far = permute_grid(half, lambda row, col: (SIDE - 1 - row, col))
    return half.astype(F32) + far.astype(F32)


def exchange(pieces, groups):
    return lax.all_to_all(pieces, "kfac", 0, 0, axis_index_groups=groups)


ROW_GROUPS = [[row * SIDE + col for col in range(SIDE)] for row in range(SIDE)]
COL_GROUPS = [[row * SIDE + col for row in range(SIDE)] for col in range(SIDE)]


def dot_nt(left, right):
    return lax.dot_general(left, right, (((1,), (1,)), ((), ())), preferred_element_type=F32)


def dot_nn(left, right):
    return lax.dot_general(left, right, (((1,), (0,)), ((), ())), preferred_element_type=F32)


def whole(count):
    return [pl.BlockSpec(memory_space=pltpu.VMEM)] * count


def cut_kernel(source_ref, out_ref):
    width = out_ref.shape[2]
    for j in range(out_ref.shape[0]):
        out_ref[j] = source_ref[:, j * width : (j + 1) * width]


def cut_columns(source, count):
    height, width = source.shape
    return pl.pallas_call(
        cut_kernel,
        in_specs=whole(1),
        out_specs=pl.BlockSpec(memory_space=pltpu.VMEM),
        out_shape=jax.ShapeDtypeStruct((count, height, width // count), source.dtype),
        cost_estimate=pl.CostEstimate(
            flops=0, bytes_accessed=4 * height * width, transcendentals=0
        ),
    )(source)


def back_kernel(shard_ref, *refs):
    out_ref = refs[-1]
    shard = shard_ref[...]
    start = 0
    for weight_ref in refs[:-1]:
        size = weight_ref.shape[0]
        out_ref[:, start : start + size] = dot_nt(shard, weight_ref[...]).astype(out_ref.dtype)
        start += size


def back_product(shard, weights):
    tokens, depth = shard.shape
    block = sum(w.shape[0] for w in weights)
    return pl.pallas_call(
        back_kernel,
        in_specs=whole(1 + len(weights)),
        out_specs=pl.BlockSpec(memory_space=pltpu.VMEM),
        out_shape=jax.ShapeDtypeStruct((tokens, block), BF),
        cost_estimate=pl.CostEstimate(
            flops=2 * tokens * depth * block,
            bytes_accessed=2 * depth * (tokens + block) + 2 * tokens * block,
            transcendentals=0,
        ),
    )(shard, *weights)


def proj_kernel(slope_ref, own_ref, ahead_ref, top_ref, bottom_ref, behind_ref, sent_ref, sum_ref):
    size = own_ref.shape[1]
    half = top_ref.shape[0]
    first = slope_ref[:, :size]
    second = slope_ref[:, size : 2 * size]
    third = slope_ref[:, 2 * size : 3 * size]
    fourth = slope_ref[:, 3 * size :]
    for start, far_ref in ((0, top_ref), (half, bottom_ref)):
        here = slice(start, start + half)
        total = dot_nt(first, own_ref[here, :]) + dot_nt(second, ahead_ref[here, :])
        total = total + dot_nt(third, far_ref[...]) + dot_nt(fourth, behind_ref[here, :])
        sum_ref[:, here] = total
        sent_ref[:, here] = total.astype(sent_ref.dtype)


def proj_product(slope, weights):
    tokens, block = slope.shape
    width = weights[0].shape[0]
    return pl.pallas_call(
        proj_kernel,
        in_specs=whole(1 + len(weights)),
        out_specs=whole(2),
        out_shape=[
            jax.ShapeDtypeStruct((tokens, width), BF),
            jax.ShapeDtypeStruct((tokens, width), F32),
        ],
        cost_estimate=pl.CostEstimate(
            flops=2 * tokens * width * block,
            bytes_accessed=2 * block * (tokens + width) + 6 * tokens * width,
            transcendentals=0,
        ),
    )(slope, *weights)


def after(value, *others):
    return lax.optimization_barrier((value,) + others)[0]


def spin_first(block):
    return from_col(block, 1), from_col(block, SIDE - 1)


def spin_second(ahead, behind):
    half = ahead.shape[0] // 2
    return from_col(ahead[:half], 1), from_col(behind[half:], SIDE - 1)


def left_kernel(block_ref, factor_ref, x_ref, out_ref):
    out_ref[...] = dot_nt(factor_ref[...], x_ref[...]).astype(out_ref.dtype)


def left_product(block_here, factor, x):
    size = factor.shape[0]
    tokens = x.shape[0]
    return pl.pallas_call(
        left_kernel,
        grid_spec=pltpu.PrefetchScalarGridSpec(
            num_scalar_prefetch=1,
            grid=(1,),
            in_specs=[
                pl.BlockSpec((size, size), lambda i, block: (0, 0)),
                pl.BlockSpec((tokens, size), lambda i, block: (0, block[0])),
            ],
            out_specs=pl.BlockSpec((size, tokens), lambda i, block: (0, 0)),
        ),
        out_shape=jax.ShapeDtypeStruct((size, tokens), BF),
        cost_estimate=pl.CostEstimate(
            flops=2 * size * size * tokens,
            bytes_accessed=2 * size * (size + 2 * tokens),
            transcendentals=0,
        ),
    )(block_here, factor, x)


def spread_kernel(slots_ref, left_ref, right_ref, out_ref):
    out_ref[...] = dot_nn(left_ref[...], right_ref[...]).astype(out_ref.dtype)


def spread(slots, left, right, height):
    depth = left.shape[1]
    width = right.shape[1]
    block_count = slots.shape[0]
    return pl.pallas_call(
        spread_kernel,
        grid_spec=pltpu.PrefetchScalarGridSpec(
            num_scalar_prefetch=1,
            grid=(block_count,),
            in_specs=[
                pl.BlockSpec((height, depth), lambda b, slots: (slots[b], 0)),
                pl.BlockSpec((depth, width), lambda b, slots: (0, 0)),
            ],
            out_specs=pl.BlockSpec((height, width), lambda b, slots: (b, 0)),
        ),
        out_shape=jax.ShapeDtypeStruct((block_count * height, width), BF),
        cost_estimate=pl.CostEstimate(
            flops=2 * block_count * height * depth * width,
            bytes_accessed=2 * block_count * height * (depth + width),
            transcendentals=0,
        ),
    )(slots, left, right)


def on_device(
    top_cotangent, inputs, proj_weight, return_weight, owners, input_inverses, output_inverses
):
    section_count = lax.axis_size("section")
    section_here = lax.axis_index("section")
    kfac_here = lax.axis_index("kfac")
    row, col = kfac_here // SIDE, kfac_here % SIDE
    core, plane = section_here % 2, section_here // 2
    odd_here = core == 1
    micro, per_micro, shard_width = top_cotangent.shape
    tokens = micro * per_micro
    group_tokens = tokens // SIDE
    x = inputs[0].reshape(tokens, -1)
    weight = proj_weight[0]
    width, stripe = weight.shape
    quarter = width // SIDE
    pair = SIDE // 2
    block_width = input_inverses.shape[2]
    block_count = width // block_width

    back_pieces = exchange(cut_columns(return_weight[0], SIDE), COL_GROUPS)
    proj_pieces = exchange(weight.reshape(SIDE, quarter, stripe), COL_GROUPS)

    def split(pieces):
        kept = lax.dynamic_slice_in_dim(pieces, pair * core, pair, 0)
        sent = lax.dynamic_slice_in_dim(pieces, pair * (1 - core), pair, 0)
        return kept, swap_cores(sent)

    def odd_even(kept, received):
        return jnp.where(odd_here, kept, received), jnp.where(odd_here, received, kept)

    def side_by_side(pieces):
        return jnp.concatenate([pieces[i] for i in range(pair)], axis=1)

    back_odd, back_even = odd_even(*[p.reshape(-1, quarter) for p in split(back_pieces)])
    proj_odd, proj_even = odd_even(*[side_by_side(p) for p in split(proj_pieces)])
    gathered = []
    ready = ()
    for block in (back_odd, proj_odd, back_even, proj_even):
        block = after(block, *ready)
        ready = spin_first(block)
        gathered.append([block, ready[0], *spin_second(*ready), ready[1]])
    chain_weights = ((gathered[0], gathered[1]), (gathered[2], gathered[3]))

    top = exchange(top_cotangent.reshape(SIDE, group_tokens, shard_width), ROW_GROUPS)
    shard = jnp.concatenate([top[i] for i in range(SIDE)], axis=1)

    slopes = silu_slope(dot_nn(x, weight)).reshape(1, SIDE, group_tokens, stripe)
    slopes = jnp.broadcast_to(slopes, (SIDE, SIDE, group_tokens, stripe))
    slopes = lax.all_to_all(slopes.reshape(SIDE * SIDE, group_tokens, stripe), "kfac", 0, 0)
    slopes = slopes.reshape(SIDE, SIDE, group_tokens, stripe)

    def in_ring_order(by_col):
        twice = jnp.concatenate([by_col, by_col], axis=1)
        return lax.dynamic_slice_in_dim(twice, col, SIDE, 1)

    factors = [
        jnp.transpose(in_ring_order(part), (2, 1, 0, 3)).reshape(group_tokens, -1)
        for part in odd_even(*split(slopes))
    ]

    group_here = row // pair
    out_rows = lax.dynamic_slice(
        output_inverses[0],
        (group_here, 0, row % pair * SIDE * stripe),
        (1, block_width, SIDE * stripe),
    ).reshape(pair, SIDE, stripe, SIDE * stripe)
    out_rows = jnp.swapaxes(in_ring_order(out_rows), 0, 1).reshape(block_width, SIDE * stripe)

    targets = owners[0] + slot_numbers(owners[0])
    mine = targets == kfac_here
    block_here = jnp.sum(jnp.where(mine, jnp.arange(block_count, dtype=jnp.int32), 0))
    left_here = left_product(block_here[None], input_inverses[0, 0], x)

    saved = None
    for visit in range(section_count // 2):
        new = []
        for factor, (back_weights, proj_weights) in zip(factors, chain_weights):
            back = sum_rows(back_product(shard, back_weights))
            slope = (back * factor).astype(BF)
            sent, own = proj_product(slope, proj_weights)
            summed = shard.astype(F32) + own + swap_cores(sent).astype(F32)
            shard = summed.astype(BF)
            new += [slope, shard]
        active = plane == section_count // 2 - 1 - visit
        saved = new if saved is None else [jnp.where(active, n, o) for n, o in zip(new, saved)]
        if visit == 0:
            left_all = lax.all_gather(after(left_here, shard), "kfac", axis=0, tiled=True)
        if visit < section_count // 2 - 1:
            shard = pass_down(shard)

    slope_odd, shard_odd, slope_even, shard_even = saved
    slope_mine = jnp.where(odd_here, slope_odd, slope_even)
    slope_other = swap_cores(jnp.where(odd_here, slope_even, slope_odd))
    slope_group = jnp.where(core == group_here, slope_mine, slope_other)
    right = dot_nn(slope_group, out_rows).astype(BF).reshape(group_tokens, SIDE, stripe)
    output = jnp.where(odd_here, shard_odd, shard_even).reshape(group_tokens, SIDE, shard_width)
    both = jnp.swapaxes(jnp.concatenate([output, right], axis=2), 0, 1)
    both = exchange(both, ROW_GROUPS).reshape(tokens, shard_width + stripe)
    outputs, right = both[:, :shard_width], both[:, shard_width:]
    result = spread(targets, left_all, right, block_width)
    return outputs.reshape(1, micro, per_micro, shard_width), result[None]


def solution(mesh):
    return jax.shard_map(
        on_device,
        mesh=mesh,
        in_specs=(
            P(None, None, "kfac"),
            P("section", None, None, None),
            P("section", None, "kfac"),
            P("section", "kfac", None),
            P("section", None),
            P("section", "kfac", None, None),
            P("section", None, None, None),
        ),
        out_specs=(P("section", None, None, "kfac"), P("section", None, "kfac")),
        check_vma=False,
    )
```

```python
import jax
import jax.numpy as jnp
from jax import lax
from jax.experimental import pallas as pl
from jax.experimental.pallas import tpu as pltpu
from jax.sharding import PartitionSpec as P

BF = jnp.bfloat16
F32 = jnp.float32
SIDE = 4


def silu_slope(values):
    sigmoid = jax.nn.sigmoid(values)
    return sigmoid * (1.0 + values * (1.0 - sigmoid))


def slot_numbers(owner_row):
    blocks = owner_row.shape[0]
    earlier = jnp.arange(blocks)[None, :] < jnp.arange(blocks)[:, None]
    shared = owner_row[None, :] == owner_row[:, None]
    return jnp.sum(jnp.logical_and(earlier, shared).astype(jnp.int32), axis=1)


def permute_grid(block, source):
    route = []
    for row in range(SIDE):
        for col in range(SIDE):
            from_row, from_col = source(row, col)
            route.append((from_row * SIDE + from_col, row * SIDE + col))
    return lax.ppermute(block, "kfac", route)


def from_col(block, distance):
    return permute_grid(block, lambda row, col: (row, (col + distance) % SIDE))


def from_row(block, distance, core):
    size = SIDE * SIDE
    route = []
    for section in range(core, lax.axis_size("section"), 2):
        for row in range(SIDE):
            for col in range(SIDE):
                source = (row + distance) % SIDE * SIDE + col
                route.append((section * size + source, section * size + row * SIDE + col))
    return lax.ppermute(block, ("section", "kfac"), route)


def to_other_core(block, core):
    sections = range(core, lax.axis_size("section"), 2)
    return lax.ppermute(block, "section", [(i, i ^ 1) for i in sections])


def swap_cores(block):
    sections = lax.axis_size("section")
    return lax.ppermute(block, "section", [(i, i ^ 1) for i in range(sections)])


def pass_down(block):
    sections = lax.axis_size("section")
    return lax.ppermute(block, "section", [(i, i - 2) for i in range(2, sections)])


def sum_rows(block):
    near = permute_grid(block, lambda row, col: (row ^ 1, col))
    half = (block.astype(F32) + near.astype(F32)).astype(BF)
    far = permute_grid(half, lambda row, col: (SIDE - 1 - row, col))
    return half.astype(F32) + far.astype(F32)


def exchange(pieces, groups):
    return lax.all_to_all(pieces, "kfac", 0, 0, axis_index_groups=groups)


ROW_GROUPS = [[row * SIDE + col for col in range(SIDE)] for row in range(SIDE)]
COL_GROUPS = [[row * SIDE + col for row in range(SIDE)] for col in range(SIDE)]


def dot_nt(left, right):
    return lax.dot_general(left, right, (((1,), (1,)), ((), ())), preferred_element_type=F32)


def dot_nn(left, right):
    return lax.dot_general(left, right, (((1,), (0,)), ((), ())), preferred_element_type=F32)


def whole(count):
    return [pl.BlockSpec(memory_space=pltpu.VMEM)] * count


def chunk(index, size):
    return pl.ds(pl.multiple_of(lax.rem(index + SIDE, SIDE) * size, size), size)


def cut(row, source, axis):
    shape = list(source.shape)
    shape[axis] //= SIDE
    size = shape[axis]

    def body(row_ref, source_ref, *outs):
        for j, out_ref in enumerate(outs):
            view = [slice(None)] * len(shape)
            view[axis] = chunk(row_ref[0] - j, size)
            out_ref[...] = source_ref[tuple(view)]

    return pl.pallas_call(
        body,
        in_specs=[pl.BlockSpec(memory_space=pltpu.SMEM)] + whole(1),
        out_specs=whole(SIDE),
        out_shape=[jax.ShapeDtypeStruct(tuple(shape), source.dtype)] * SIDE,
        cost_estimate=pl.CostEstimate(
            flops=0, bytes_accessed=4 * source.size, transcendentals=0
        ),
    )(row[None], source)


def after(value, *others):
    return lax.optimization_barrier((value,) + others)[0]


def spin_first(block):
    return from_col(block, 1), from_col(block, SIDE - 1)


def spin_second(ahead, behind):
    half = ahead.shape[0] // 2
    return from_col(ahead[:half], 1), from_col(behind[half:], SIDE - 1)


def left_kernel(block_ref, factor_ref, x_ref, out_ref):
    out_ref[...] = dot_nt(factor_ref[...], x_ref[...]).astype(out_ref.dtype)


def left_product(block_here, factor, x):
    size = factor.shape[0]
    tokens = x.shape[0]
    return pl.pallas_call(
        left_kernel,
        grid_spec=pltpu.PrefetchScalarGridSpec(
            num_scalar_prefetch=1,
            grid=(1,),
            in_specs=[
                pl.BlockSpec((size, size), lambda i, block: (0, 0)),
                pl.BlockSpec((tokens, size), lambda i, block: (0, block[0])),
            ],
            out_specs=pl.BlockSpec((size, tokens), lambda i, block: (0, 0)),
        ),
        out_shape=jax.ShapeDtypeStruct((size, tokens), BF),
        cost_estimate=pl.CostEstimate(
            flops=2 * size * size * tokens,
            bytes_accessed=2 * size * (size + 2 * tokens),
            transcendentals=0,
        ),
    )(block_here, factor, x)


def on_device(
    top_cotangent, inputs, proj_weight, return_weight, owners, input_inverses, output_inverses
):
    section_count = lax.axis_size("section")
    section_here = lax.axis_index("section")
    kfac_here = lax.axis_index("kfac")
    row, col = kfac_here // SIDE, kfac_here % SIDE
    core, plane = section_here % 2, section_here // 2
    odd_here = core == 1
    micro, per_micro, shard_width = top_cotangent.shape
    tokens = micro * per_micro
    group_tokens = tokens // SIDE
    x = inputs[0].reshape(tokens, -1)
    weight = proj_weight[0]
    width, stripe = weight.shape
    quarter = width // SIDE
    pair = SIDE // 2
    block_width = input_inverses.shape[2]
    block_count = width // block_width

    cuts = [cut(row, return_weight[0], 1), cut(row, weight, 0)]
    picks = [lax.rem(place - row + SIDE, SIDE) for place in range(SIDE)]
    gathered = []
    exchanged = ()
    ready = ()
    for core_now in (1, 0):
        for axis, pieces in enumerate(cuts):
            exchanged = [
                from_row(after(pieces[j], *exchanged), j, core_now) for j in range(1, SIDE)
            ]
            parts = [pieces[0]] + exchanged
            groups = [
                jnp.concatenate([lax.select_n(p, *parts) for p in picks[i : i + pair]], axis=axis)
                for i in range(0, SIDE, pair)
            ]
            block = jnp.where(
                core == core_now,
                groups[core_now],
                to_other_core(groups[1 - core_now], core_now),
            )
            block = after(block, *ready)
            ready = spin_first(block)
            far = jnp.concatenate(spin_second(*ready), axis=0)
            gathered.append(jnp.concatenate([block, ready[0], far, ready[1]], axis=axis))
    chain_weights = ((gathered[0], gathered[1]), (gathered[2], gathered[3]))

    def split(pieces):
        kept = lax.dynamic_slice_in_dim(pieces, pair * core, pair, 0)
        sent = lax.dynamic_slice_in_dim(pieces, pair * (1 - core), pair, 0)
        return kept, swap_cores(sent)

    def odd_even(kept, received):
        return jnp.where(odd_here, kept, received), jnp.where(odd_here, received, kept)

    top = exchange(top_cotangent.reshape(SIDE, group_tokens, shard_width), ROW_GROUPS)
    shard = jnp.concatenate([top[i] for i in range(SIDE)], axis=1)

    slopes = silu_slope(dot_nn(x, weight)).reshape(1, SIDE, group_tokens, stripe)
    slopes = jnp.broadcast_to(slopes, (SIDE, SIDE, group_tokens, stripe))
    slopes = lax.all_to_all(slopes.reshape(SIDE * SIDE, group_tokens, stripe), "kfac", 0, 0)
    slopes = slopes.reshape(SIDE, SIDE, group_tokens, stripe)

    def in_ring_order(by_col):
        twice = jnp.concatenate([by_col, by_col], axis=1)
        return lax.dynamic_slice_in_dim(twice, col, SIDE, 1)

    factors = [
        jnp.transpose(in_ring_order(part), (2, 1, 0, 3)).reshape(group_tokens, -1)
        for part in odd_even(*split(slopes))
    ]

    group_here = row // pair
    out_rows = lax.dynamic_slice(
        output_inverses[0],
        (group_here, 0, row % pair * SIDE * stripe),
        (1, block_width, SIDE * stripe),
    ).reshape(pair, SIDE, stripe, SIDE * stripe)
    out_rows = jnp.swapaxes(in_ring_order(out_rows), 0, 1).reshape(block_width, SIDE * stripe)

    targets = owners[0] + slot_numbers(owners[0])
    mine = targets == kfac_here
    block_here = jnp.sum(jnp.where(mine, jnp.arange(block_count, dtype=jnp.int32), 0))
    left_here = left_product(block_here[None], input_inverses[0, 0], x)

    saved = None
    for visit in range(section_count // 2):
        new = []
        for factor, (back_now, proj_now) in zip(factors, chain_weights):
            back = sum_rows(dot_nt(shard, back_now).astype(BF))
            slope = (back * factor).astype(BF)
            own = dot_nt(slope, proj_now)
            summed = shard.astype(F32) + own + swap_cores(own.astype(BF)).astype(F32)
            shard = summed.astype(BF)
            new += [slope, shard]
        active = plane == section_count // 2 - 1 - visit
        saved = new if saved is None else [jnp.where(active, n, o) for n, o in zip(new, saved)]
        if visit == 0:
            left_all = lax.all_gather(after(left_here, shard), "kfac", axis=0, tiled=True)
        if visit < section_count // 2 - 1:
            shard = pass_down(shard)

    left = jnp.concatenate(
        [
            lax.dynamic_slice_in_dim(left_all, targets[b] * block_width, block_width, 0)
            for b in range(block_count)
        ]
    )

    slope_odd, shard_odd, slope_even, shard_even = saved
    slope_mine = jnp.where(odd_here, slope_odd, slope_even)
    slope_other = swap_cores(jnp.where(odd_here, slope_even, slope_odd))
    slope_group = jnp.where(core == group_here, slope_mine, slope_other)
    right = dot_nn(slope_group, out_rows).astype(BF).reshape(group_tokens, SIDE, stripe)
    output = jnp.where(odd_here, shard_odd, shard_even).reshape(group_tokens, SIDE, shard_width)
    both = jnp.swapaxes(jnp.concatenate([output, right], axis=2), 0, 1)
    both = exchange(both, ROW_GROUPS).reshape(tokens, shard_width + stripe)
    outputs, right = both[:, :shard_width], both[:, shard_width:]
    result = dot_nn(left, right).astype(BF)
    return outputs.reshape(1, micro, per_micro, shard_width), result[None]


def solution(mesh):
    return jax.shard_map(
        on_device,
        mesh=mesh,
        in_specs=(
            P(None, None, "kfac"),
            P("section", None, None, None),
            P("section", None, "kfac"),
            P("section", "kfac", None),
            P("section", None),
            P("section", "kfac", None, None),
            P("section", None, None, None),
        ),
        out_specs=(P("section", None, None, "kfac"), P("section", None, "kfac")),
        check_vma=False,
    )
```

```python
import jax
import jax.numpy as jnp
from jax import lax
from jax.experimental import pallas as pl
from jax.experimental.pallas import tpu as pltpu
from jax.sharding import PartitionSpec as P

BF = jnp.bfloat16
F32 = jnp.float32
SIDE = 4


def silu_slope(values):
    sigmoid = jax.nn.sigmoid(values)
    return sigmoid * (1.0 + values * (1.0 - sigmoid))


def slot_numbers(owner_row):
    blocks = owner_row.shape[0]
    earlier = jnp.arange(blocks)[None, :] < jnp.arange(blocks)[:, None]
    shared = owner_row[None, :] == owner_row[:, None]
    return jnp.sum(jnp.logical_and(earlier, shared).astype(jnp.int32), axis=1)


def permute_grid(block, source):
    route = []
    for row in range(SIDE):
        for col in range(SIDE):
            from_row, from_col = source(row, col)
            route.append((from_row * SIDE + from_col, row * SIDE + col))
    return lax.ppermute(block, "kfac", route)


def from_col(block, distance):
    return permute_grid(block, lambda row, col: (row, (col + distance) % SIDE))


def from_row(block, distance, core):
    size = SIDE * SIDE
    route = []
    for section in range(core, lax.axis_size("section"), 2):
        for row in range(SIDE):
            for col in range(SIDE):
                source = (row + distance) % SIDE * SIDE + col
                route.append((section * size + source, section * size + row * SIDE + col))
    return lax.ppermute(block, ("section", "kfac"), route)


def to_other_core(block, core):
    sections = range(core, lax.axis_size("section"), 2)
    return lax.ppermute(block, "section", [(i, i ^ 1) for i in sections])


def swap_cores(block):
    sections = lax.axis_size("section")
    return lax.ppermute(block, "section", [(i, i ^ 1) for i in range(sections)])


def pass_down(block):
    sections = lax.axis_size("section")
    return lax.ppermute(block, "section", [(i, i - 2) for i in range(2, sections)])


def sum_rows(block):
    near = permute_grid(block, lambda row, col: (row ^ 1, col))
    half = (block.astype(F32) + near.astype(F32)).astype(BF)
    far = permute_grid(half, lambda row, col: (SIDE - 1 - row, col))
    return half.astype(F32) + far.astype(F32)


def exchange(pieces, groups):
    return lax.all_to_all(pieces, "kfac", 0, 0, axis_index_groups=groups)


ROW_GROUPS = [[row * SIDE + col for col in range(SIDE)] for row in range(SIDE)]
COL_GROUPS = [[row * SIDE + col for row in range(SIDE)] for col in range(SIDE)]


def dot_nt(left, right):
    return lax.dot_general(left, right, (((1,), (1,)), ((), ())), preferred_element_type=F32)


def dot_nn(left, right):
    return lax.dot_general(left, right, (((1,), (0,)), ((), ())), preferred_element_type=F32)


def whole(count):
    return [pl.BlockSpec(memory_space=pltpu.VMEM)] * count


def chunk(index, size):
    return pl.ds(pl.multiple_of(lax.rem(index + SIDE, SIDE) * size, size), size)


def cut(row, source, axis):
    shape = list(source.shape)
    shape[axis] //= SIDE
    size = shape[axis]

    def body(row_ref, source_ref, *outs):
        for j, out_ref in enumerate(outs):
            view = [slice(None)] * len(shape)
            view[axis] = chunk(row_ref[0] - j, size)
            out_ref[...] = source_ref[tuple(view)]

    return pl.pallas_call(
        body,
        in_specs=[pl.BlockSpec(memory_space=pltpu.SMEM)] + whole(1),
        out_specs=whole(SIDE),
        out_shape=[jax.ShapeDtypeStruct(tuple(shape), source.dtype)] * SIDE,
        cost_estimate=pl.CostEstimate(
            flops=0, bytes_accessed=4 * source.size, transcendentals=0
        ),
    )(row[None], source)


def after(value, *others):
    return lax.optimization_barrier((value,) + others)[0]


def spin_first(block):
    return from_col(block, 1), from_col(block, SIDE - 1)


def spin_second(ahead, behind):
    half = ahead.shape[0] // 2
    return from_col(ahead[:half], 1), from_col(behind[half:], SIDE - 1)


def left_kernel(block_ref, factor_ref, x_ref, out_ref):
    out_ref[...] = dot_nt(factor_ref[...], x_ref[...]).astype(out_ref.dtype)


def left_product(block_here, factor, x):
    size = factor.shape[0]
    tokens = x.shape[0]
    return pl.pallas_call(
        left_kernel,
        grid_spec=pltpu.PrefetchScalarGridSpec(
            num_scalar_prefetch=1,
            grid=(1,),
            in_specs=[
                pl.BlockSpec((size, size), lambda i, block: (0, 0)),
                pl.BlockSpec((tokens, size), lambda i, block: (0, block[0])),
            ],
            out_specs=pl.BlockSpec((size, tokens), lambda i, block: (0, 0)),
        ),
        out_shape=jax.ShapeDtypeStruct((size, tokens), BF),
        cost_estimate=pl.CostEstimate(
            flops=2 * size * size * tokens,
            bytes_accessed=2 * size * (size + 2 * tokens),
            transcendentals=0,
        ),
    )(block_here, factor, x)


def join(axis, own, ahead, far, behind):
    size = own.shape[axis]
    shape = list(own.shape)
    shape[axis] *= SIDE
    whole_block = jnp.zeros(tuple(shape), own.dtype)
    starts = [(0, 0), (0, size), (0, 3 * size), (0, 2 * size), (far[0].shape[0], 2 * size)]
    if axis == 0:
        starts = [(0, 0), (size, 0), (3 * size, 0), (2 * size, 0), (2 * size + size // 2, 0)]
    for part, start in zip((own, ahead, behind) + tuple(far), starts):
        whole_block = lax.dynamic_update_slice(whole_block, part, start)
    return whole_block


def on_device(
    top_cotangent, inputs, proj_weight, return_weight, owners, input_inverses, output_inverses
):
    section_count = lax.axis_size("section")
    section_here = lax.axis_index("section")
    kfac_here = lax.axis_index("kfac")
    row, col = kfac_here // SIDE, kfac_here % SIDE
    core, plane = section_here % 2, section_here // 2
    odd_here = core == 1
    micro, per_micro, shard_width = top_cotangent.shape
    tokens = micro * per_micro
    group_tokens = tokens // SIDE
    x = inputs[0].reshape(tokens, -1)
    weight = proj_weight[0]
    width, stripe = weight.shape
    quarter = width // SIDE
    pair = SIDE // 2
    block_width = input_inverses.shape[2]
    block_count = width // block_width

    slopes = silu_slope(dot_nn(x, weight)).astype(BF).reshape(1, SIDE, group_tokens, stripe)
    slopes = jnp.broadcast_to(slopes, (SIDE, SIDE, group_tokens, stripe))
    slopes = lax.all_to_all(slopes.reshape(SIDE * SIDE, group_tokens, stripe), "kfac", 0, 0)
    slopes = slopes.reshape(SIDE, SIDE, group_tokens, stripe)

    cuts = [cut(row, return_weight[0], 1), cut(row, weight, 0)]
    picks = [lax.rem(place - row + SIDE, SIDE) for place in range(SIDE)]
    gathered = []
    exchanged = ()
    held = [()]
    far = ()
    for core_now in (1, 0):
        for axis, pieces in enumerate(cuts):
            exchanged = [
                from_row(after(pieces[j], *exchanged, *held[-1]), j, core_now)
                for j in range(1, SIDE)
            ]
            parts = [pieces[0]] + exchanged
            if not gathered:
                parts[0] = after(parts[0], slopes)
            groups = [
                jnp.concatenate([lax.select_n(p, *parts) for p in picks[i : i + pair]], axis=axis)
                for i in range(0, SIDE, pair)
            ]
            block = jnp.where(
                core == core_now,
                groups[core_now],
                to_other_core(groups[1 - core_now], core_now),
            )
            if not gathered:
                first_block = block
            held.append(far if gathered else (block,))
            block = after(block, *far)
            near = spin_first(block)
            far = spin_second(*near)
            gathered.append(join(axis, block, near[0], far, near[1]))
    chain_weights = ((gathered[0], gathered[1]), (gathered[2], gathered[3]))

    def split(pieces):
        kept = lax.dynamic_slice_in_dim(pieces, pair * core, pair, 0)
        sent = lax.dynamic_slice_in_dim(pieces, pair * (1 - core), pair, 0)
        return kept, swap_cores(sent)

    def odd_even(kept, received):
        return jnp.where(odd_here, kept, received), jnp.where(odd_here, received, kept)

    top = after(top_cotangent.reshape(SIDE, group_tokens, shard_width), first_block)
    top = exchange(top, ROW_GROUPS)
    shard = jnp.concatenate([top[i] for i in range(SIDE)], axis=1)

    def in_ring_order(by_col):
        twice = jnp.concatenate([by_col, by_col], axis=1)
        return lax.dynamic_slice_in_dim(twice, col, SIDE, 1)

    factors = [
        jnp.transpose(in_ring_order(part), (2, 1, 0, 3)).reshape(group_tokens, -1)
        for part in odd_even(*split(slopes))
    ]

    group_here = row // pair
    out_rows = lax.dynamic_slice(
        output_inverses[0],
        (group_here, 0, row % pair * SIDE * stripe),
        (1, block_width, SIDE * stripe),
    ).reshape(pair, SIDE, stripe, SIDE * stripe)
    out_rows = jnp.swapaxes(in_ring_order(out_rows), 0, 1).reshape(block_width, SIDE * stripe)

    targets = owners[0] + slot_numbers(owners[0])
    mine = targets == kfac_here
    block_here = jnp.sum(jnp.where(mine, jnp.arange(block_count, dtype=jnp.int32), 0))
    left_here = left_product(block_here[None], input_inverses[0, 0], x)

    saved = None
    for visit in range(section_count // 2):
        new = []
        for factor, (back_now, proj_now) in zip(factors, chain_weights):
            back = sum_rows(dot_nt(shard, back_now).astype(BF))
            slope = (back * factor).astype(BF)
            own = dot_nt(slope, proj_now)
            summed = shard.astype(F32) + own + swap_cores(own.astype(BF)).astype(F32)
            shard = summed.astype(BF)
            new += [slope, shard]
        active = plane == section_count // 2 - 1 - visit
        saved = new if saved is None else [jnp.where(active, n, o) for n, o in zip(new, saved)]
        if visit == 0:
            left_all = lax.all_gather(after(left_here, shard), "kfac", axis=0, tiled=True)
            left = jnp.concatenate(
                [
                    lax.dynamic_slice_in_dim(left_all, targets[i] * block_width, block_width, 0)
                    for i in range(block_count)
                ]
            )
        if visit < section_count // 2 - 1:
            shard = pass_down(shard)
        if visit == section_count // 2 - 2:
            shard, left = lax.optimization_barrier((shard, left))

    slope_odd, shard_odd, slope_even, shard_even = saved
    slope_mine = jnp.where(odd_here, slope_odd, slope_even)
    slope_other = swap_cores(jnp.where(odd_here, slope_even, slope_odd))
    slope_group = jnp.where(core == group_here, slope_mine, slope_other)
    right = dot_nn(slope_group, out_rows).astype(BF).reshape(group_tokens, SIDE, stripe)
    output = jnp.where(odd_here, shard_odd, shard_even).reshape(group_tokens, SIDE, shard_width)
    both = jnp.swapaxes(jnp.concatenate([output, right], axis=2), 0, 1)
    both = exchange(both, ROW_GROUPS).reshape(tokens, shard_width + stripe)
    outputs, right = both[:, :shard_width], both[:, shard_width:]
    result = dot_nn(left, right).astype(BF)
    return outputs.reshape(1, micro, per_micro, shard_width), result[None]


def solution(mesh):
    return jax.shard_map(
        on_device,
        mesh=mesh,
        in_specs=(
            P(None, None, "kfac"),
            P("section", None, None, None),
            P("section", None, "kfac"),
            P("section", "kfac", None),
            P("section", None),
            P("section", "kfac", None, None),
            P("section", None, None, None),
        ),
        out_specs=(P("section", None, None, "kfac"), P("section", None, "kfac")),
        check_vma=False,
    )
```

```python
import jax
import jax.numpy as jnp
from jax import lax
from jax.experimental import pallas as pl
from jax.experimental.pallas import tpu as pltpu
from jax.sharding import PartitionSpec as P

BF = jnp.bfloat16
F32 = jnp.float32
SIDE = 4


def silu_slope(values):
    sigmoid = jax.nn.sigmoid(values)
    return sigmoid * (1.0 + values * (1.0 - sigmoid))


def slot_numbers(owner_row):
    blocks = owner_row.shape[0]
    earlier = jnp.arange(blocks)[None, :] < jnp.arange(blocks)[:, None]
    shared = owner_row[None, :] == owner_row[:, None]
    return jnp.sum(jnp.logical_and(earlier, shared).astype(jnp.int32), axis=1)


def permute_grid(block, source):
    route = []
    for row in range(SIDE):
        for col in range(SIDE):
            from_row, from_col = source(row, col)
            route.append((from_row * SIDE + from_col, row * SIDE + col))
    return lax.ppermute(block, "kfac", route)


def from_col(block, distance):
    return permute_grid(block, lambda row, col: (row, (col + distance) % SIDE))


def from_row(block, distance, core):
    size = SIDE * SIDE
    route = []
    for section in range(core, lax.axis_size("section"), 2):
        for row in range(SIDE):
            for col in range(SIDE):
                source = (row + distance) % SIDE * SIDE + col
                route.append((section * size + source, section * size + row * SIDE + col))
    return lax.ppermute(block, ("section", "kfac"), route)


def to_other_core(block, core):
    sections = range(core, lax.axis_size("section"), 2)
    return lax.ppermute(block, "section", [(i, i ^ 1) for i in sections])


def swap_cores(block):
    sections = lax.axis_size("section")
    return lax.ppermute(block, "section", [(i, i ^ 1) for i in range(sections)])


def pass_down(block):
    sections = lax.axis_size("section")
    return lax.ppermute(block, "section", [(i, i - 2) for i in range(2, sections)])


def sum_rows(block):
    copies = jnp.broadcast_to(block[None], (SIDE,) + block.shape)
    return jnp.sum(exchange(copies, COL_GROUPS).astype(F32), axis=0)


def exchange(pieces, groups):
    return lax.all_to_all(pieces, "kfac", 0, 0, axis_index_groups=groups)


ROW_GROUPS = [[row * SIDE + col for col in range(SIDE)] for row in range(SIDE)]
COL_GROUPS = [[row * SIDE + col for row in range(SIDE)] for col in range(SIDE)]


def dot_nt(left, right):
    return lax.dot_general(left, right, (((1,), (1,)), ((), ())), preferred_element_type=F32)


def dot_nn(left, right):
    return lax.dot_general(left, right, (((1,), (0,)), ((), ())), preferred_element_type=F32)


def whole(count):
    return [pl.BlockSpec(memory_space=pltpu.VMEM)] * count


def chunk(index, size):
    return pl.ds(pl.multiple_of(lax.rem(index + SIDE, SIDE) * size, size), size)


def cut(row, returning, weight):
    stripe, width = returning.shape
    quarter = width // SIDE

    def body(row_ref, returning_ref, weight_ref, *outs):
        for j, out_ref in enumerate(outs):
            here = chunk(row_ref[0] - j, quarter)
            out_ref[:stripe, :] = returning_ref[:, here]
            out_ref[stripe:, :] = weight_ref[here, :].T

    return pl.pallas_call(
        body,
        in_specs=[pl.BlockSpec(memory_space=pltpu.SMEM)] + whole(2),
        out_specs=whole(SIDE),
        out_shape=[jax.ShapeDtypeStruct((2 * stripe, quarter), weight.dtype)] * SIDE,
        cost_estimate=pl.CostEstimate(
            flops=0, bytes_accessed=8 * stripe * width, transcendentals=0
        ),
    )(row[None], returning, weight)


def after(value, *others):
    return lax.optimization_barrier((value,) + others)[0]


def spin_first(block):
    return from_col(block, 1), from_col(block, SIDE - 1)


def spin_second(ahead, behind):
    half = ahead.shape[0] // 2
    return from_col(ahead[:half], 1), from_col(behind[half:], SIDE - 1)


def left_kernel(block_ref, factor_ref, x_ref, out_ref):
    out_ref[...] = dot_nt(factor_ref[...], x_ref[...]).astype(out_ref.dtype)


def left_product(block_here, factor, x):
    size = factor.shape[0]
    tokens = x.shape[0]
    return pl.pallas_call(
        left_kernel,
        grid_spec=pltpu.PrefetchScalarGridSpec(
            num_scalar_prefetch=1,
            grid=(1,),
            in_specs=[
                pl.BlockSpec((size, size), lambda i, block: (0, 0)),
                pl.BlockSpec((tokens, size), lambda i, block: (0, block[0])),
            ],
            out_specs=pl.BlockSpec((size, tokens), lambda i, block: (0, 0)),
        ),
        out_shape=jax.ShapeDtypeStruct((size, tokens), BF),
        cost_estimate=pl.CostEstimate(
            flops=2 * size * size * tokens,
            bytes_accessed=2 * size * (size + 2 * tokens),
            transcendentals=0,
        ),
    )(block_here, factor, x)


def join(own, ahead, far, behind):
    size, width = own.shape
    joined = jnp.zeros((SIDE * size, width), own.dtype)
    starts = (0, size, 3 * size, 2 * size, 2 * size + size // 2)
    for part, start in zip((own, ahead, behind) + tuple(far), starts):
        joined = lax.dynamic_update_slice(joined, part, (start, 0))
    return joined


def on_device(
    top_cotangent, inputs, proj_weight, return_weight, owners, input_inverses, output_inverses
):
    section_count = lax.axis_size("section")
    section_here = lax.axis_index("section")
    kfac_here = lax.axis_index("kfac")
    row, col = kfac_here // SIDE, kfac_here % SIDE
    core, plane = section_here % 2, section_here // 2
    odd_here = core == 1
    micro, per_micro, shard_width = top_cotangent.shape
    tokens = micro * per_micro
    group_tokens = tokens // SIDE
    x = inputs[0].reshape(tokens, -1)
    weight = proj_weight[0]
    width, stripe = weight.shape
    quarter = width // SIDE
    pair = SIDE // 2
    block_width = input_inverses.shape[2]
    block_count = width // block_width

    top = exchange(top_cotangent.reshape(SIDE, group_tokens, shard_width), ROW_GROUPS)

    slopes = silu_slope(dot_nn(x, weight)).astype(BF).reshape(1, SIDE, group_tokens, stripe)
    slopes = jnp.broadcast_to(slopes, (SIDE, SIDE, group_tokens, stripe))
    slopes = lax.all_to_all(slopes.reshape(SIDE * SIDE, group_tokens, stripe), "kfac", 0, 0)

    pieces = cut(row, return_weight[0], weight)
    picks = [lax.rem(place - row + SIDE, SIDE) for place in range(SIDE)]
    gathered = []
    held = near = far = ()
    for core_now in (1, 0):
        parts = [pieces[0]] + [
            from_row(after(pieces[j], *held), j, core_now) for j in range(1, SIDE)
        ]
        parts[0] = after(parts[0], *(far if held else (top, slopes)))
        for kind in (0, 1):
            rows = [part[kind * stripe : (kind + 1) * stripe] for part in parts]
            if kind:
                rows[0] = after(rows[0], block)
            groups = [
                jnp.concatenate([lax.select_n(p, *rows) for p in picks[i : i + pair]])
                for i in range(0, SIDE, pair)
            ]
            block = jnp.where(
                core == core_now,
                after(groups[core_now], *near),
                to_other_core(groups[1 - core_now], core_now),
            )
            near = spin_first(block)
            last = spin_second(*near)
            far = far or last
            gathered.append(join(block, near[0], last, near[1]))
        held = (block,)
    chain_weights = ((gathered[0], gathered[1]), (gathered[2], gathered[3]))

    top = top.reshape(SIDE, group_tokens, shard_width)
    shard = jnp.concatenate([top[i] for i in range(SIDE)], axis=1)
    slopes = slopes.reshape(SIDE, SIDE, group_tokens, stripe)

    def split(pieces):
        kept = lax.dynamic_slice_in_dim(pieces, pair * core, pair, 0)
        sent = lax.dynamic_slice_in_dim(pieces, pair * (1 - core), pair, 0)
        return kept, swap_cores(sent)

    def odd_even(kept, received):
        return jnp.where(odd_here, kept, received), jnp.where(odd_here, received, kept)

    def in_ring_order(by_col):
        twice = jnp.concatenate([by_col, by_col], axis=1)
        return lax.dynamic_slice_in_dim(twice, col, SIDE, 1)

    factors = [
        jnp.transpose(in_ring_order(part), (2, 1, 0, 3)).reshape(group_tokens, -1)
        for part in odd_even(*split(slopes))
    ]

    group_here = row // pair
    out_rows = lax.dynamic_slice(
        output_inverses[0],
        (group_here, 0, row % pair * SIDE * stripe),
        (1, block_width, SIDE * stripe),
    ).reshape(pair, SIDE, stripe, SIDE * stripe)
    out_rows = jnp.swapaxes(in_ring_order(out_rows), 0, 1).reshape(block_width, SIDE * stripe)

    targets = owners[0] + slot_numbers(owners[0])
    mine = targets == kfac_here
    block_here = jnp.sum(jnp.where(mine, jnp.arange(block_count, dtype=jnp.int32), 0))
    left_here = left_product(block_here[None], input_inverses[0, 0], x)

    saved = None
    for visit in range(section_count // 2):
        new = []
        for factor, (back_now, proj_now) in zip(factors, chain_weights):
            back = sum_rows(dot_nt(shard, back_now).astype(BF))
            slope = (back * factor).astype(BF)
            own = dot_nn(slope, proj_now)
            summed = shard.astype(F32) + own + swap_cores(own.astype(BF)).astype(F32)
            shard = summed.astype(BF)
            new += [slope, shard]
        active = plane == section_count // 2 - 1 - visit
        saved = new if saved is None else [jnp.where(active, n, o) for n, o in zip(new, saved)]
        if visit == 0:
            left_all = lax.all_gather(after(left_here, shard), "kfac", axis=0, tiled=True)
            left = jnp.concatenate(
                [
                    lax.dynamic_slice_in_dim(left_all, targets[i] * block_width, block_width, 0)
                    for i in range(block_count)
                ]
            )
        if visit < section_count // 2 - 1:
            shard = pass_down(shard)
        if visit == section_count // 2 - 2:
            shard, left = lax.optimization_barrier((shard, left))

    slope_odd, shard_odd, slope_even, shard_even = saved
    slope_mine = jnp.where(odd_here, slope_odd, slope_even)
    slope_other = swap_cores(jnp.where(odd_here, slope_even, slope_odd))
    slope_group = jnp.where(core == group_here, slope_mine, slope_other)
    right = dot_nn(slope_group, out_rows).astype(BF).reshape(group_tokens, SIDE, stripe)
    output = jnp.where(odd_here, shard_odd, shard_even).reshape(group_tokens, SIDE, shard_width)
    both = jnp.swapaxes(jnp.concatenate([output, right], axis=2), 0, 1)
    both = exchange(both, ROW_GROUPS).reshape(tokens, shard_width + stripe)
    outputs, right = both[:, :shard_width], both[:, shard_width:]
    result = dot_nn(left, right).astype(BF)
    return outputs.reshape(1, micro, per_micro, shard_width), result[None]


def solution(mesh):
    return jax.shard_map(
        on_device,
        mesh=mesh,
        in_specs=(
            P(None, None, "kfac"),
            P("section", None, None, None),
            P("section", None, "kfac"),
            P("section", "kfac", None),
            P("section", None),
            P("section", "kfac", None, None),
            P("section", None, None, None),
        ),
        out_specs=(P("section", None, None, "kfac"), P("section", None, "kfac")),
        check_vma=False,
    )
```

```python
import jax
import jax.numpy as jnp
from jax import lax
from jax.experimental import pallas as pl
from jax.experimental.pallas import tpu as pltpu
from jax.sharding import PartitionSpec as P

BF = jnp.bfloat16
F32 = jnp.float32
SIDE = 4


def silu_slope(values):
    sigmoid = jax.nn.sigmoid(values)
    return sigmoid * (1.0 + values * (1.0 - sigmoid))


def slot_numbers(owner_row):
    blocks = owner_row.shape[0]
    earlier = jnp.arange(blocks)[None, :] < jnp.arange(blocks)[:, None]
    shared = owner_row[None, :] == owner_row[:, None]
    return jnp.sum(jnp.logical_and(earlier, shared).astype(jnp.int32), axis=1)


def permute_grid(block, source):
    route = []
    for row in range(SIDE):
        for col in range(SIDE):
            from_row, from_col = source(row, col)
            route.append((from_row * SIDE + from_col, row * SIDE + col))
    return lax.ppermute(block, "kfac", route)


def from_col(block, distance):
    return permute_grid(block, lambda row, col: (row, (col + distance) % SIDE))


def from_row(block, distance, core):
    size = SIDE * SIDE
    route = []
    for section in range(core, lax.axis_size("section"), 2):
        for row in range(SIDE):
            for col in range(SIDE):
                source = (row + distance) % SIDE * SIDE + col
                route.append((section * size + source, section * size + row * SIDE + col))
    return lax.ppermute(block, ("section", "kfac"), route)


def to_other_core(block, core):
    sections = range(core, lax.axis_size("section"), 2)
    return lax.ppermute(block, "section", [(i, i ^ 1) for i in sections])


def swap_cores(block):
    sections = lax.axis_size("section")
    return lax.ppermute(block, "section", [(i, i ^ 1) for i in range(sections)])


def pass_down(block):
    sections = lax.axis_size("section")
    return lax.ppermute(block, "section", [(i, i - 2) for i in range(2, sections)])


def sum_rows(block):
    near = permute_grid(block, lambda row, col: (row ^ 1, col))
    half = (block.astype(F32) + near.astype(F32)).astype(BF)
    far = permute_grid(half, lambda row, col: (SIDE - 1 - row, col))
    return half.astype(F32) + far.astype(F32)


def exchange(pieces, groups):
    return lax.all_to_all(pieces, "kfac", 0, 0, axis_index_groups=groups)


ROW_GROUPS = [[row * SIDE + col for col in range(SIDE)] for row in range(SIDE)]
COL_GROUPS = [[row * SIDE + col for row in range(SIDE)] for col in range(SIDE)]


def dot_nt(left, right):
    return lax.dot_general(left, right, (((1,), (1,)), ((), ())), preferred_element_type=F32)


def dot_nn(left, right):
    return lax.dot_general(left, right, (((1,), (0,)), ((), ())), preferred_element_type=F32)


def whole(count):
    return [pl.BlockSpec(memory_space=pltpu.VMEM)] * count


def chunk(index, size):
    return pl.ds(pl.multiple_of(lax.rem(index + SIDE, SIDE) * size, size), size)


def cut(row, returning, weight):
    stripe, width = returning.shape
    quarter = width // SIDE

    def body(row_ref, returning_ref, weight_ref, *outs):
        for j, out_ref in enumerate(outs):
            here = chunk(row_ref[0] - j, quarter)
            out_ref[:stripe, :] = returning_ref[:, here]
            out_ref[stripe:, :] = weight_ref[here, :].T

    return pl.pallas_call(
        body,
        in_specs=[pl.BlockSpec(memory_space=pltpu.SMEM)] + whole(2),
        out_specs=whole(SIDE),
        out_shape=[jax.ShapeDtypeStruct((2 * stripe, quarter), weight.dtype)] * SIDE,
        cost_estimate=pl.CostEstimate(
            flops=0, bytes_accessed=8 * stripe * width, transcendentals=0
        ),
    )(row[None], returning, weight)


def after(value, *others):
    return lax.optimization_barrier((value,) + others)[0]


def spin_first(block):
    return from_col(block, 1), from_col(block, SIDE - 1)


def spin_second(ahead, behind):
    half = ahead.shape[0] // 2
    return from_col(ahead[:half], 1), from_col(behind[half:], SIDE - 1)


def left_kernel(block_ref, factor_ref, x_ref, out_ref):
    out_ref[...] = dot_nt(factor_ref[...], x_ref[...]).astype(out_ref.dtype)


def left_product(block_here, factor, x):
    size = factor.shape[0]
    tokens = x.shape[0]
    return pl.pallas_call(
        left_kernel,
        grid_spec=pltpu.PrefetchScalarGridSpec(
            num_scalar_prefetch=1,
            grid=(1,),
            in_specs=[
                pl.BlockSpec((size, size), lambda i, block: (0, 0)),
                pl.BlockSpec((tokens, size), lambda i, block: (0, block[0])),
            ],
            out_specs=pl.BlockSpec((size, tokens), lambda i, block: (0, 0)),
        ),
        out_shape=jax.ShapeDtypeStruct((size, tokens), BF),
        cost_estimate=pl.CostEstimate(
            flops=2 * size * size * tokens,
            bytes_accessed=2 * size * (size + 2 * tokens),
            transcendentals=0,
        ),
    )(block_here, factor, x)


def spread_kernel(slots_ref, *refs):
    lefts, right_ref, out_ref = refs[:SIDE], refs[SIDE], refs[SIDE + 1]
    size = lefts[0].shape[0]
    for i, left_ref in enumerate(lefts):
        product = dot_nn(left_ref[...], right_ref[...])
        out_ref[i * size : (i + 1) * size, :] = product.astype(out_ref.dtype)


def spread(slots, left, right, height):
    depth = left.shape[1]
    width = right.shape[1]
    block_count = slots.shape[0]
    part = height // SIDE
    streams = [
        pl.BlockSpec((part, depth), lambda b, slots, i=i: (slots[b] * SIDE + i, 0))
        for i in range(SIDE)
    ]
    return pl.pallas_call(
        spread_kernel,
        grid_spec=pltpu.PrefetchScalarGridSpec(
            num_scalar_prefetch=1,
            grid=(block_count,),
            in_specs=streams + [pl.BlockSpec((depth, width), lambda b, slots: (0, 0))],
            out_specs=pl.BlockSpec((height, width), lambda b, slots: (b, 0)),
        ),
        out_shape=jax.ShapeDtypeStruct((block_count * height, width), BF),
        cost_estimate=pl.CostEstimate(
            flops=2 * block_count * height * depth * width,
            bytes_accessed=2 * block_count * height * (depth + width),
            transcendentals=0,
        ),
    )(slots, *[left] * SIDE, right)


def join(own, ahead, far, behind):
    size, width = own.shape
    joined = jnp.zeros((SIDE * size, width), own.dtype)
    starts = (0, size, 3 * size, 2 * size, 2 * size + size // 2)
    for part, start in zip((own, ahead, behind) + tuple(far), starts):
        joined = lax.dynamic_update_slice(joined, part, (start, 0))
    return joined


def on_device(
    top_cotangent, inputs, proj_weight, return_weight, owners, input_inverses, output_inverses
):
    section_count = lax.axis_size("section")
    section_here = lax.axis_index("section")
    kfac_here = lax.axis_index("kfac")
    row, col = kfac_here // SIDE, kfac_here % SIDE
    core, plane = section_here % 2, section_here // 2
    odd_here = core == 1
    micro, per_micro, shard_width = top_cotangent.shape
    tokens = micro * per_micro
    group_tokens = tokens // SIDE
    x = inputs[0].reshape(tokens, -1)
    weight = proj_weight[0]
    width, stripe = weight.shape
    quarter = width // SIDE
    pair = SIDE // 2
    block_width = input_inverses.shape[2]
    block_count = width // block_width

    top = exchange(top_cotangent.reshape(SIDE, group_tokens, shard_width), ROW_GROUPS)

    slopes = silu_slope(dot_nn(x, weight)).astype(BF).reshape(1, SIDE, group_tokens, stripe)
    slopes = jnp.broadcast_to(slopes, (SIDE, SIDE, group_tokens, stripe))
    slopes = lax.all_to_all(slopes.reshape(SIDE * SIDE, group_tokens, stripe), "kfac", 0, 0)

    pieces = cut(row, return_weight[0], weight)
    picks = [lax.rem(place - row + SIDE, SIDE) for place in range(SIDE)]

    def exchange_rows(core_now, first, last, *held):
        own = [after(piece, *held)[first:last] for piece in pieces]
        return own[:1] + [from_row(own[j], j, core_now) for j in range(1, SIDE)]

    def core_block(rows, core_now, gate, *held):
        rows = [after(rows[0], *gate)] + rows[1:]
        groups = [
            jnp.concatenate([lax.select_n(p, *rows) for p in picks[i : i + pair]])
            for i in range(0, SIDE, pair)
        ]
        received = to_other_core(groups[1 - core_now], core_now)
        return jnp.where(core == core_now, after(groups[core_now], *held), received)

    def spin(block):
        near = spin_first(block)
        return near, join(block, near[0], spin_second(*near), near[1])

    odd = exchange_rows(1, 0, 2 * stripe)
    block = core_block([part[:stripe] for part in odd], 1, (top, slopes))
    even_back = exchange_rows(0, 0, stripe, block)
    near_back, back_odd = spin(block)
    block = core_block([part[stripe:] for part in odd], 1, (block,), *near_back, *even_back[1:])
    even_proj = exchange_rows(0, stripe, 2 * stripe, block)
    near_proj, proj_odd = spin(block)
    block = core_block(even_back, 0, (block,), *near_proj, *even_proj[1:])
    near_even, back_even = spin(block)
    block = core_block(even_proj, 0, (block,), *near_even)
    near_last, proj_even = spin(block)
    gates = [near_proj, near_even, near_last, ()]
    chain_weights = ((back_odd, proj_odd), (back_even, proj_even))

    top = top.reshape(SIDE, group_tokens, shard_width)
    shard = jnp.concatenate([top[i] for i in range(SIDE)], axis=1)
    slopes = after(slopes, *near_proj).reshape(SIDE, SIDE, group_tokens, stripe)

    def split(pieces):
        kept = lax.dynamic_slice_in_dim(pieces, pair * core, pair, 0)
        sent = lax.dynamic_slice_in_dim(pieces, pair * (1 - core), pair, 0)
        return kept, swap_cores(sent)

    def odd_even(kept, received):
        return jnp.where(odd_here, kept, received), jnp.where(odd_here, received, kept)

    def in_ring_order(by_col):
        twice = jnp.concatenate([by_col, by_col], axis=1)
        return lax.dynamic_slice_in_dim(twice, col, SIDE, 1)

    factors = [
        jnp.transpose(in_ring_order(part), (2, 1, 0, 3)).reshape(group_tokens, -1)
        for part in odd_even(*split(slopes))
    ]

    group_here = row // pair
    out_rows = lax.dynamic_slice(
        output_inverses[0],
        (group_here, 0, row % pair * SIDE * stripe),
        (1, block_width, SIDE * stripe),
    ).reshape(pair, SIDE, stripe, SIDE * stripe)
    out_rows = jnp.swapaxes(in_ring_order(out_rows), 0, 1).reshape(block_width, SIDE * stripe)

    targets = owners[0] + slot_numbers(owners[0])
    mine = targets == kfac_here
    block_here = jnp.sum(jnp.where(mine, jnp.arange(block_count, dtype=jnp.int32), 0))
    left_here = left_product(block_here[None], input_inverses[0, 0], x)

    saved = None
    for visit in range(section_count // 2):
        new = []
        for factor, (back_now, proj_now) in zip(factors, chain_weights):
            if visit == 0:
                shard = after(shard, *gates.pop(0))
            back = sum_rows(dot_nt(shard, back_now).astype(BF))
            slope = (back * factor).astype(BF)
            if visit == 0:
                slope = after(slope, *gates.pop(0))
            own = dot_nn(slope, proj_now)
            summed = shard.astype(F32) + own + swap_cores(own.astype(BF)).astype(F32)
            shard = summed.astype(BF)
            new += [slope, shard]
        active = plane == section_count // 2 - 1 - visit
        saved = new if saved is None else [jnp.where(active, n, o) for n, o in zip(new, saved)]
        if visit == 0:
            left_all = lax.all_gather(after(left_here, shard), "kfac", axis=0, tiled=True)
        if visit < section_count // 2 - 1:
            shard = pass_down(shard)

    slope_odd, shard_odd, slope_even, shard_even = saved
    slope_mine = jnp.where(odd_here, slope_odd, slope_even)
    slope_other = swap_cores(jnp.where(odd_here, slope_even, slope_odd))
    slope_group = jnp.where(core == group_here, slope_mine, slope_other)
    right = dot_nn(slope_group, out_rows).astype(BF).reshape(group_tokens, SIDE, stripe)
    output = jnp.where(odd_here, shard_odd, shard_even).reshape(group_tokens, SIDE, shard_width)
    both = jnp.swapaxes(jnp.concatenate([output, right], axis=2), 0, 1)
    both = exchange(both, ROW_GROUPS).reshape(tokens, shard_width + stripe)
    outputs, right = both[:, :shard_width], both[:, shard_width:]
    result = spread(targets, left_all, right, block_width)
    return outputs.reshape(1, micro, per_micro, shard_width), result[None]


def solution(mesh):
    return jax.shard_map(
        on_device,
        mesh=mesh,
        in_specs=(
            P(None, None, "kfac"),
            P("section", None, None, None),
            P("section", None, "kfac"),
            P("section", "kfac", None),
            P("section", None),
            P("section", "kfac", None, None),
            P("section", None, None, None),
        ),
        out_specs=(P("section", None, None, "kfac"), P("section", None, "kfac")),
        check_vma=False,
    )
```

```python
import jax
import jax.numpy as jnp
from jax import lax
from jax.experimental import pallas as pl
from jax.experimental.pallas import tpu as pltpu
from jax.sharding import PartitionSpec as P

BF = jnp.bfloat16
F32 = jnp.float32
SIDE = 4


def silu_slope(values):
    sigmoid = jax.nn.sigmoid(values)
    return sigmoid * (1.0 + values * (1.0 - sigmoid))


def slot_numbers(owner_row):
    blocks = owner_row.shape[0]
    earlier = jnp.arange(blocks)[None, :] < jnp.arange(blocks)[:, None]
    shared = owner_row[None, :] == owner_row[:, None]
    return jnp.sum(jnp.logical_and(earlier, shared).astype(jnp.int32), axis=1)


def permute_grid(block, source):
    route = []
    for row in range(SIDE):
        for col in range(SIDE):
            from_row, from_col = source(row, col)
            route.append((from_row * SIDE + from_col, row * SIDE + col))
    return lax.ppermute(block, "kfac", route)


def from_col(block, distance):
    return permute_grid(block, lambda row, col: (row, (col + distance) % SIDE))


def from_row(block, distance, core):
    size = SIDE * SIDE
    route = []
    for section in range(core, lax.axis_size("section"), 2):
        for row in range(SIDE):
            for col in range(SIDE):
                source = (row + distance) % SIDE * SIDE + col
                route.append((section * size + source, section * size + row * SIDE + col))
    return lax.ppermute(block, ("section", "kfac"), route)


def to_other_core(block, core):
    sections = range(core, lax.axis_size("section"), 2)
    return lax.ppermute(block, "section", [(i, i ^ 1) for i in sections])


def swap_cores(block):
    sections = lax.axis_size("section")
    return lax.ppermute(block, "section", [(i, i ^ 1) for i in range(sections)])


def pass_down(block):
    sections = lax.axis_size("section")
    return lax.ppermute(block, "section", [(i, i - 2) for i in range(2, sections)])


def sum_rows(block):
    near = permute_grid(block, lambda row, col: (row ^ 1, col))
    half = (block.astype(F32) + near.astype(F32)).astype(BF)
    far = permute_grid(half, lambda row, col: (SIDE - 1 - row, col))
    return half.astype(F32) + far.astype(F32)


def exchange(pieces, groups):
    return lax.all_to_all(pieces, "kfac", 0, 0, axis_index_groups=groups)


ROW_GROUPS = [[row * SIDE + col for col in range(SIDE)] for row in range(SIDE)]
COL_GROUPS = [[row * SIDE + col for row in range(SIDE)] for col in range(SIDE)]


def dot_nt(left, right):
    return lax.dot_general(left, right, (((1,), (1,)), ((), ())), preferred_element_type=F32)


def dot_nn(left, right):
    return lax.dot_general(left, right, (((1,), (0,)), ((), ())), preferred_element_type=F32)


def whole(count):
    return [pl.BlockSpec(memory_space=pltpu.VMEM)] * count


def chunk(index, size):
    return pl.ds(pl.multiple_of(lax.rem(index + SIDE, SIDE) * size, size), size)


def cut(row, returning, weight):
    stripe, width = returning.shape
    quarter = width // SIDE

    def body(row_ref, returning_ref, weight_ref, *outs):
        for j, out_ref in enumerate(outs):
            here = chunk(row_ref[0] - j, quarter)
            out_ref[:stripe, :] = returning_ref[:, here]
            out_ref[stripe:, :] = weight_ref[here, :].T

    return pl.pallas_call(
        body,
        in_specs=[pl.BlockSpec(memory_space=pltpu.SMEM)] + whole(2),
        out_specs=whole(SIDE),
        out_shape=[jax.ShapeDtypeStruct((2 * stripe, quarter), weight.dtype)] * SIDE,
        cost_estimate=pl.CostEstimate(
            flops=0, bytes_accessed=8 * stripe * width, transcendentals=0
        ),
    )(row[None], returning, weight)


def after(value, *others):
    return lax.optimization_barrier((value,) + others)[0]


def left_kernel(block_ref, factor_ref, x_ref, out_ref):
    out_ref[...] = dot_nt(factor_ref[...], x_ref[...]).astype(out_ref.dtype)


def left_product(block_here, factor, x):
    size = factor.shape[0]
    tokens = x.shape[0]
    return pl.pallas_call(
        left_kernel,
        grid_spec=pltpu.PrefetchScalarGridSpec(
            num_scalar_prefetch=1,
            grid=(1,),
            in_specs=[
                pl.BlockSpec((size, size), lambda i, block: (0, 0)),
                pl.BlockSpec((tokens, size), lambda i, block: (0, block[0])),
            ],
            out_specs=pl.BlockSpec((size, tokens), lambda i, block: (0, 0)),
        ),
        out_shape=jax.ShapeDtypeStruct((size, tokens), BF),
        cost_estimate=pl.CostEstimate(
            flops=2 * size * size * tokens,
            bytes_accessed=2 * size * (size + 2 * tokens),
            transcendentals=0,
        ),
    )(block_here, factor, x)


def spread_kernel(slots_ref, *refs):
    lefts, right_ref, out_ref = refs[:SIDE], refs[SIDE], refs[SIDE + 1]
    size = lefts[0].shape[0]
    for i, left_ref in enumerate(lefts):
        product = dot_nn(left_ref[...], right_ref[...])
        out_ref[i * size : (i + 1) * size, :] = product.astype(out_ref.dtype)


def spread(slots, left, right, height):
    depth = left.shape[1]
    width = right.shape[1]
    block_count = slots.shape[0]
    streams = [
        pl.BlockSpec(
            (height // 2, depth), lambda b, slots, i=i: (slots[2 * b + i // 2] * 2 + i % 2, 0)
        )
        for i in range(SIDE)
    ]
    return pl.pallas_call(
        spread_kernel,
        grid_spec=pltpu.PrefetchScalarGridSpec(
            num_scalar_prefetch=1,
            grid=(block_count // 2,),
            in_specs=streams + [pl.BlockSpec((depth, width), lambda b, slots: (0, 0))],
            out_specs=pl.BlockSpec((2 * height, width), lambda b, slots: (b, 0)),
        ),
        out_shape=jax.ShapeDtypeStruct((block_count * height, width), BF),
        cost_estimate=pl.CostEstimate(
            flops=2 * block_count * height * depth * width,
            bytes_accessed=2 * block_count * height * (depth + width),
            transcendentals=0,
        ),
    )(slots, *[left] * SIDE, right)


def join(own, ahead, far, behind):
    size, width = own.shape
    joined = jnp.zeros((SIDE * size, width), own.dtype)
    starts = (0, size, 3 * size, 2 * size, 2 * size + size // 2)
    for part, start in zip((own, ahead, behind) + tuple(far), starts):
        joined = lax.dynamic_update_slice(joined, part, (start, 0))
    return joined


def on_device(
    top_cotangent, inputs, proj_weight, return_weight, owners, input_inverses, output_inverses
):
    section_count = lax.axis_size("section")
    section_here = lax.axis_index("section")
    kfac_here = lax.axis_index("kfac")
    row, col = kfac_here // SIDE, kfac_here % SIDE
    core, plane = section_here % 2, section_here // 2
    odd_here = core == 1
    micro, per_micro, shard_width = top_cotangent.shape
    tokens = micro * per_micro
    group_tokens = tokens // SIDE
    x = inputs[0].reshape(tokens, -1)
    weight = proj_weight[0]
    width, stripe = weight.shape
    quarter = width // SIDE
    pair = SIDE // 2
    block_width = input_inverses.shape[2]
    block_count = width // block_width

    top = exchange(top_cotangent.reshape(SIDE, group_tokens, shard_width), ROW_GROUPS)

    slopes = silu_slope(dot_nn(x, weight)).astype(BF).reshape(1, SIDE, group_tokens, stripe)
    slopes = jnp.broadcast_to(slopes, (SIDE, SIDE, group_tokens, stripe))
    slopes = lax.all_to_all(slopes.reshape(SIDE * SIDE, group_tokens, stripe), "kfac", 0, 0)

    pieces = cut(row, return_weight[0], weight)
    picks = [lax.rem(place - row + SIDE, SIDE) for place in range(SIDE)]

    def exchange_rows(core_now, first, last, *held):
        own = [after(piece, *held)[first:last] for piece in pieces]
        return own[:1] + [from_row(own[j], j, core_now) for j in range(1, SIDE)]

    def core_groups(rows, core_now, *gate):
        rows = [after(rows[0], *gate)] + rows[1:]
        groups = [
            jnp.concatenate([lax.select_n(p, *rows) for p in picks[i : i + pair]])
            for i in range(0, SIDE, pair)
        ]
        return groups[core_now], to_other_core(groups[1 - core_now], core_now)

    half = stripe
    odd = exchange_rows(1, 0, 2 * stripe)
    kept, received = core_groups([part[:stripe] for part in odd], 1, top, slopes)
    block = jnp.where(core == 1, kept, received)
    ahead, behind = from_col(block, 1), from_col(block, SIDE - 1)
    kept, received = core_groups([part[stripe:] for part in odd], 1, block)
    even = exchange_rows(0, 0, 2 * stripe, *odd[1:])
    before = even[1:]
    sent = []
    gathered = []
    for core_now in (1, 0, 0, None):
        back_half = (ahead[:half], behind[half:])
        last, near = block, (ahead, behind)
        if core_now is None:
            far = (from_col(back_half[0], 1), from_col(back_half[1], SIDE - 1))
        else:
            block = jnp.where(core == core_now, after(kept, ahead, behind, *before), received)
            before = []
            sent.append([jnp.concatenate([part, block]) for part in back_half])
            ahead, behind = from_col(sent[-1][0], 1), from_col(sent[-1][1], SIDE - 1)
            far = (ahead[:half], behind[:half])
            ahead, behind = ahead[half:], behind[half:]
            if len(gathered) < 2:
                kind = len(gathered) * stripe
                rows = [part[kind : kind + stripe] for part in even]
                kept, received = core_groups(rows, 0, block)
        gathered.append(join(last, near[0], far, near[1]))
    back_odd, proj_odd, back_even, proj_even = gathered
    chain_weights = ((back_odd, proj_odd), (back_even, proj_even))

    top = top.reshape(SIDE, group_tokens, shard_width)
    shard = jnp.concatenate([top[i] for i in range(SIDE)], axis=1)
    slopes = after(slopes, back_odd).reshape(SIDE, SIDE, group_tokens, stripe)

    def split(pieces):
        kept = lax.dynamic_slice_in_dim(pieces, pair * core, pair, 0)
        sent = lax.dynamic_slice_in_dim(pieces, pair * (1 - core), pair, 0)
        return kept, swap_cores(sent)

    def odd_even(kept, received):
        return jnp.where(odd_here, kept, received), jnp.where(odd_here, received, kept)

    def in_ring_order(by_col):
        twice = jnp.concatenate([by_col, by_col], axis=1)
        return lax.dynamic_slice_in_dim(twice, col, SIDE, 1)

    factors = [
        jnp.transpose(in_ring_order(part), (2, 1, 0, 3)).reshape(group_tokens, -1)
        for part in odd_even(*split(slopes))
    ]

    group_here = row // pair
    out_rows = lax.dynamic_slice(
        output_inverses[0],
        (group_here, 0, row % pair * SIDE * stripe),
        (1, block_width, SIDE * stripe),
    ).reshape(pair, SIDE, stripe, SIDE * stripe)
    out_rows = jnp.swapaxes(in_ring_order(out_rows), 0, 1).reshape(block_width, SIDE * stripe)

    targets = owners[0] + slot_numbers(owners[0])
    mine = targets == kfac_here
    block_here = jnp.sum(jnp.where(mine, jnp.arange(block_count, dtype=jnp.int32), 0))
    left_here = left_product(block_here[None], input_inverses[0, 0], x)

    saved = None
    for visit in range(section_count // 2):
        new = []
        for factor, (back_now, proj_now) in zip(factors, chain_weights):
            if visit == 0 and not new:
                shard = after(shard, *sent[1])
            back = sum_rows(dot_nt(shard, back_now).astype(BF))
            slope = (back * factor).astype(BF)
            if visit == 0 and not new:
                slope = after(slope, *sent[2])
            own = dot_nn(slope, proj_now)
            summed = shard.astype(F32) + own + swap_cores(own.astype(BF)).astype(F32)
            shard = summed.astype(BF)
            new += [slope, shard]
        active = plane == section_count // 2 - 1 - visit
        saved = new if saved is None else [jnp.where(active, n, o) for n, o in zip(new, saved)]
        if visit == 0:
            left_all = lax.all_gather(after(left_here, shard), "kfac", axis=0, tiled=True)
        if visit < section_count // 2 - 1:
            shard = pass_down(shard)

    slope_odd, shard_odd, slope_even, shard_even = saved
    slope_mine = jnp.where(odd_here, slope_odd, slope_even)
    slope_other = swap_cores(jnp.where(odd_here, slope_even, slope_odd))
    slope_group = jnp.where(core == group_here, slope_mine, slope_other)
    right = dot_nn(slope_group, out_rows).astype(BF).reshape(group_tokens, SIDE, stripe)
    right = exchange(jnp.swapaxes(right, 0, 1), ROW_GROUPS).reshape(tokens, stripe)
    output = jnp.where(odd_here, shard_odd, shard_even).reshape(group_tokens, SIDE, shard_width)
    outputs = exchange(after(jnp.swapaxes(output, 0, 1), right), ROW_GROUPS)
    result = spread(targets, left_all, right, block_width)
    return outputs.reshape(1, micro, per_micro, shard_width), result[None]


def solution(mesh):
    return jax.shard_map(
        on_device,
        mesh=mesh,
        in_specs=(
            P(None, None, "kfac"),
            P("section", None, None, None),
            P("section", None, "kfac"),
            P("section", "kfac", None),
            P("section", None),
            P("section", "kfac", None, None),
            P("section", None, None, None),
        ),
        out_specs=(P("section", None, None, "kfac"), P("section", None, "kfac")),
        check_vma=False,
    )
```

```python
import jax
import jax.numpy as jnp
from jax import lax
from jax.experimental import pallas as pl
from jax.experimental.pallas import tpu as pltpu
from jax.sharding import PartitionSpec as P

BF = jnp.bfloat16
F32 = jnp.float32
SIDE = 4


def silu_slope(values):
    sigmoid = jax.nn.sigmoid(values)
    return sigmoid * (1.0 + values * (1.0 - sigmoid))


def slot_numbers(owner_row):
    blocks = owner_row.shape[0]
    earlier = jnp.arange(blocks)[None, :] < jnp.arange(blocks)[:, None]
    shared = owner_row[None, :] == owner_row[:, None]
    return jnp.sum(jnp.logical_and(earlier, shared).astype(jnp.int32), axis=1)


def permute_grid(block, source):
    route = []
    for row in range(SIDE):
        for col in range(SIDE):
            from_row, from_col = source(row, col)
            route.append((from_row * SIDE + from_col, row * SIDE + col))
    return lax.ppermute(block, "kfac", route)


def from_col(block, distance):
    return permute_grid(block, lambda row, col: (row, (col + distance) % SIDE))


def from_row(block, distance, core):
    size = SIDE * SIDE
    route = []
    for section in range(core, lax.axis_size("section"), 2):
        for row in range(SIDE):
            for col in range(SIDE):
                source = (row + distance) % SIDE * SIDE + col
                route.append((section * size + source, section * size + row * SIDE + col))
    return lax.ppermute(block, ("section", "kfac"), route)


def to_other_core(block, core):
    sections = range(core, lax.axis_size("section"), 2)
    return lax.ppermute(block, "section", [(i, i ^ 1) for i in sections])


def swap_cores(block):
    sections = lax.axis_size("section")
    return lax.ppermute(block, "section", [(i, i ^ 1) for i in range(sections)])


def pass_down(block):
    sections = lax.axis_size("section")
    return lax.ppermute(block, "section", [(i, i - 2) for i in range(2, sections)])


def sum_rows(block):
    near = permute_grid(block, lambda row, col: (row ^ 1, col))
    half = (block.astype(F32) + near.astype(F32)).astype(BF)
    far = permute_grid(half, lambda row, col: (SIDE - 1 - row, col))
    return half.astype(F32) + far.astype(F32)


def exchange(pieces, groups):
    return lax.all_to_all(pieces, "kfac", 0, 0, axis_index_groups=groups)


ROW_GROUPS = [[row * SIDE + col for col in range(SIDE)] for row in range(SIDE)]
COL_GROUPS = [[row * SIDE + col for row in range(SIDE)] for col in range(SIDE)]


def dot_nt(left, right):
    return lax.dot_general(left, right, (((1,), (1,)), ((), ())), preferred_element_type=F32)


def dot_nn(left, right):
    return lax.dot_general(left, right, (((1,), (0,)), ((), ())), preferred_element_type=F32)


def whole(count):
    return [pl.BlockSpec(memory_space=pltpu.VMEM)] * count


def chunk(index, size):
    return pl.ds(pl.multiple_of(lax.rem(index + SIDE, SIDE) * size, size), size)


def cut(row, returning, weight):
    stripe, width = returning.shape
    quarter = width // SIDE

    def body(row_ref, returning_ref, weight_ref, *outs):
        for j, out_ref in enumerate(outs):
            here = chunk(row_ref[0] - j, quarter)
            out_ref[:stripe, :] = returning_ref[:, here]
            out_ref[stripe:, :] = weight_ref[here, :].T

    return pl.pallas_call(
        body,
        in_specs=[pl.BlockSpec(memory_space=pltpu.SMEM)] + whole(2),
        out_specs=whole(SIDE),
        out_shape=[jax.ShapeDtypeStruct((2 * stripe, quarter), weight.dtype)] * SIDE,
        cost_estimate=pl.CostEstimate(
            flops=0, bytes_accessed=8 * stripe * width, transcendentals=0
        ),
    )(row[None], returning, weight)


def after(value, *others):
    return lax.optimization_barrier((value,) + others)[0]


def left_kernel(block_ref, factor_ref, x_ref, out_ref):
    out_ref[...] = dot_nt(factor_ref[...], x_ref[...]).astype(out_ref.dtype)


def left_product(block_here, factor, x):
    size = factor.shape[0]
    tokens = x.shape[0]
    return pl.pallas_call(
        left_kernel,
        grid_spec=pltpu.PrefetchScalarGridSpec(
            num_scalar_prefetch=1,
            grid=(1,),
            in_specs=[
                pl.BlockSpec((size, size), lambda i, block: (0, 0)),
                pl.BlockSpec((tokens, size), lambda i, block: (0, block[0])),
            ],
            out_specs=pl.BlockSpec((size, tokens), lambda i, block: (0, 0)),
        ),
        out_shape=jax.ShapeDtypeStruct((size, tokens), BF),
        cost_estimate=pl.CostEstimate(
            flops=2 * size * size * tokens,
            bytes_accessed=2 * size * (size + 2 * tokens),
            transcendentals=0,
        ),
    )(block_here, factor, x)


def spread_kernel(slots_ref, *refs):
    lefts, right_ref, out_ref = refs[:SIDE], refs[SIDE], refs[SIDE + 1]
    size = lefts[0].shape[0]
    for i, left_ref in enumerate(lefts):
        product = dot_nn(left_ref[...], right_ref[...])
        out_ref[i * size : (i + 1) * size, :] = product.astype(out_ref.dtype)


def spread(slots, left, right, height):
    depth = left.shape[1]
    width = right.shape[1]
    block_count = slots.shape[0]
    streams = [
        pl.BlockSpec(
            (height // 2, depth), lambda b, slots, i=i: (slots[2 * b + i // 2] * 2 + i % 2, 0)
        )
        for i in range(SIDE)
    ]
    return pl.pallas_call(
        spread_kernel,
        grid_spec=pltpu.PrefetchScalarGridSpec(
            num_scalar_prefetch=1,
            grid=(block_count // 2,),
            in_specs=streams + [pl.BlockSpec((depth, width), lambda b, slots: (0, 0))],
            out_specs=pl.BlockSpec((2 * height, width), lambda b, slots: (b, 0)),
        ),
        out_shape=jax.ShapeDtypeStruct((block_count * height, width), BF),
        cost_estimate=pl.CostEstimate(
            flops=2 * block_count * height * depth * width,
            bytes_accessed=2 * block_count * height * (depth + width),
            transcendentals=0,
        ),
    )(slots, *[left] * SIDE, right)


def join(own, ahead, far, behind):
    size, width = own.shape
    joined = jnp.zeros((SIDE * size, width), own.dtype)
    starts = (0, size, 3 * size, 2 * size, 2 * size + size // 2)
    for part, start in zip((own, ahead, behind) + tuple(far), starts):
        joined = lax.dynamic_update_slice(joined, part, (start, 0))
    return joined


def on_device(
    top_cotangent, inputs, proj_weight, return_weight, owners, input_inverses, output_inverses
):
    section_count = lax.axis_size("section")
    section_here = lax.axis_index("section")
    kfac_here = lax.axis_index("kfac")
    row, col = kfac_here // SIDE, kfac_here % SIDE
    core, plane = section_here % 2, section_here // 2
    odd_here = core == 1
    micro, per_micro, shard_width = top_cotangent.shape
    tokens = micro * per_micro
    group_tokens = tokens // SIDE
    x = inputs[0].reshape(tokens, -1)
    weight = proj_weight[0]
    width, stripe = weight.shape
    quarter = width // SIDE
    pair = SIDE // 2
    block_width = input_inverses.shape[2]
    block_count = width // block_width

    top = exchange(top_cotangent.reshape(SIDE, group_tokens, shard_width), ROW_GROUPS)

    slopes = silu_slope(dot_nn(x, weight)).astype(BF).reshape(1, SIDE, group_tokens, stripe)
    slopes = jnp.broadcast_to(slopes, (SIDE, SIDE, group_tokens, stripe))
    slopes = lax.all_to_all(slopes.reshape(SIDE * SIDE, group_tokens, stripe), "kfac", 0, 0)

    def odd_even(kept, received):
        return jnp.where(odd_here, kept, received), jnp.where(odd_here, received, kept)

    def in_ring_order(by_col):
        twice = jnp.concatenate([by_col, by_col], axis=1)
        return lax.dynamic_slice_in_dim(twice, col, SIDE, 1)

    def chain_factors(slopes):
        slopes = slopes.reshape(SIDE, SIDE, group_tokens, stripe)
        kept = lax.dynamic_slice_in_dim(slopes, pair * core, pair, 0)
        sent = lax.dynamic_slice_in_dim(slopes, pair * (1 - core), pair, 0)
        return [
            jnp.transpose(in_ring_order(part), (2, 1, 0, 3)).reshape(group_tokens, -1)
            for part in odd_even(kept, swap_cores(sent))
        ]

    pieces = cut(row, return_weight[0], weight)
    picks = [lax.rem(place - row + SIDE, SIDE) for place in range(SIDE)]

    def exchange_rows(core_now, first, last, *held):
        own = [after(piece, *held)[first:last] for piece in pieces]
        return own[:1] + [from_row(own[j], j, core_now) for j in range(1, SIDE)]

    def core_groups(rows, core_now, *gate):
        rows = [after(rows[0], *gate)] + rows[1:]
        groups = [
            jnp.concatenate([lax.select_n(p, *rows) for p in picks[i : i + pair]])
            for i in range(0, SIDE, pair)
        ]
        return groups[core_now], to_other_core(groups[1 - core_now], core_now)

    half = stripe
    odd = exchange_rows(1, 0, 2 * stripe)
    kept, received = core_groups([part[:stripe] for part in odd], 1, top, slopes)
    block = jnp.where(core == 1, kept, received)
    ahead, behind = from_col(block, 1), from_col(block, SIDE - 1)
    kept, received = core_groups([part[stripe:] for part in odd], 1, block)
    even = exchange_rows(0, 0, 2 * stripe, *odd[1:])
    before = even[1:]
    sent = []
    gathered = []
    for core_now in (1, 0, 0, None):
        back_half = (ahead[:half], behind[half:])
        last, near = block, (ahead, behind)
        if core_now is None:
            far = (from_col(back_half[0], 1), from_col(back_half[1], SIDE - 1))
        else:
            block = jnp.where(core == core_now, after(kept, ahead, behind, *before), received)
            sent.append([jnp.concatenate([part, block]) for part in back_half])
            ahead, behind = from_col(sent[-1][0], 1), from_col(sent[-1][1], SIDE - 1)
            before = []
            if len(sent) == 1:
                before = factors = chain_factors(after(slopes, *sent[0]))
            far = (ahead[:half], behind[:half])
            ahead, behind = ahead[half:], behind[half:]
            if len(gathered) < 2:
                kind = len(gathered) * stripe
                rows = [part[kind : kind + stripe] for part in even]
                kept, received = core_groups(rows, 0, block)
        gathered.append(join(last, near[0], far, near[1]))
    back_odd, proj_odd, back_even, proj_even = gathered
    chain_weights = ((back_odd, proj_odd), (back_even, proj_even))

    top = top.reshape(SIDE, group_tokens, shard_width)
    shard = jnp.concatenate([top[i] for i in range(SIDE)], axis=1)

    group_here = row // pair
    out_rows = lax.dynamic_slice(
        output_inverses[0],
        (group_here, 0, row % pair * SIDE * stripe),
        (1, block_width, SIDE * stripe),
    ).reshape(pair, SIDE, stripe, SIDE * stripe)
    out_rows = jnp.swapaxes(in_ring_order(out_rows), 0, 1).reshape(block_width, SIDE * stripe)

    targets = owners[0] + slot_numbers(owners[0])
    mine = targets == kfac_here
    block_here = jnp.sum(jnp.where(mine, jnp.arange(block_count, dtype=jnp.int32), 0))
    left_here = left_product(block_here[None], input_inverses[0, 0], x)

    saved = None
    for visit in range(section_count // 2):
        new = []
        for factor, (back_now, proj_now) in zip(factors, chain_weights):
            if visit == 0:
                shard = after(shard, left_here) if new else after(shard, *sent[1])
            back = sum_rows(dot_nt(shard, back_now).astype(BF))
            slope = (back * factor).astype(BF)
            if visit == 0 and not new:
                slope = after(slope, *sent[2])
            own = dot_nn(slope, proj_now)
            summed = shard.astype(F32) + own + swap_cores(own.astype(BF)).astype(F32)
            shard = summed.astype(BF)
            new += [slope, shard]
        active = plane == section_count // 2 - 1 - visit
        saved = new if saved is None else [jnp.where(active, n, o) for n, o in zip(new, saved)]
        if visit == 0:
            left_all = lax.all_gather(after(left_here, shard), "kfac", axis=0, tiled=True)
        if visit < section_count // 2 - 1:
            shard = pass_down(shard)

    slope_odd, shard_odd, slope_even, shard_even = saved
    slope_mine = jnp.where(odd_here, slope_odd, slope_even)
    slope_other = swap_cores(jnp.where(odd_here, slope_even, slope_odd))
    slope_group = jnp.where(core == group_here, slope_mine, slope_other)
    right = dot_nn(slope_group, out_rows).astype(BF).reshape(group_tokens, SIDE, stripe)
    output = jnp.where(odd_here, shard_odd, shard_even).reshape(group_tokens, SIDE, shard_width)
    both = jnp.swapaxes(jnp.concatenate([output, right], axis=2), 0, 1)
    both = exchange(both, ROW_GROUPS).reshape(tokens, shard_width + stripe)
    outputs, right = both[:, :shard_width], both[:, shard_width:]
    result = spread(targets, left_all, right, block_width)
    return outputs.reshape(1, micro, per_micro, shard_width), result[None]


def solution(mesh):
    return jax.shard_map(
        on_device,
        mesh=mesh,
        in_specs=(
            P(None, None, "kfac"),
            P("section", None, None, None),
            P("section", None, "kfac"),
            P("section", "kfac", None),
            P("section", None),
            P("section", "kfac", None, None),
            P("section", None, None, None),
        ),
        out_specs=(P("section", None, None, "kfac"), P("section", None, "kfac")),
        check_vma=False,
    )
```

```python
import jax
import jax.numpy as jnp
from jax import lax
from jax.experimental import pallas as pl
from jax.experimental.pallas import tpu as pltpu
from jax.sharding import PartitionSpec as P

BF = jnp.bfloat16
F32 = jnp.float32
SIDE = 4


def silu_slope(values):
    sigmoid = jax.nn.sigmoid(values)
    return sigmoid * (1.0 + values * (1.0 - sigmoid))


def slot_numbers(owner_row):
    blocks = owner_row.shape[0]
    earlier = jnp.arange(blocks)[None, :] < jnp.arange(blocks)[:, None]
    shared = owner_row[None, :] == owner_row[:, None]
    return jnp.sum(jnp.logical_and(earlier, shared).astype(jnp.int32), axis=1)


def permute_grid(block, source):
    route = []
    for row in range(SIDE):
        for col in range(SIDE):
            from_row, from_col = source(row, col)
            route.append((from_row * SIDE + from_col, row * SIDE + col))
    return lax.ppermute(block, "kfac", route)


def from_col(block, distance):
    return permute_grid(block, lambda row, col: (row, (col + distance) % SIDE))


def from_row(block, distance, core):
    size = SIDE * SIDE
    route = []
    for section in range(core, lax.axis_size("section"), 2):
        for row in range(SIDE):
            for col in range(SIDE):
                source = (row + distance) % SIDE * SIDE + col
                route.append((section * size + source, section * size + row * SIDE + col))
    return lax.ppermute(block, ("section", "kfac"), route)


def to_other_core(block, core):
    sections = range(core, lax.axis_size("section"), 2)
    return lax.ppermute(block, "section", [(i, i ^ 1) for i in sections])


def swap_cores(block):
    sections = lax.axis_size("section")
    return lax.ppermute(block, "section", [(i, i ^ 1) for i in range(sections)])


def pass_down(block):
    sections = lax.axis_size("section")
    return lax.ppermute(block, "section", [(i, i - 2) for i in range(2, sections)])


def sum_rows(block):
    near = permute_grid(block, lambda row, col: (row ^ 1, col))
    half = (block.astype(F32) + near.astype(F32)).astype(BF)
    far = permute_grid(half, lambda row, col: (SIDE - 1 - row, col))
    return half.astype(F32) + far.astype(F32)


def exchange(pieces, groups):
    return lax.all_to_all(pieces, "kfac", 0, 0, axis_index_groups=groups)


ROW_GROUPS = [[row * SIDE + col for col in range(SIDE)] for row in range(SIDE)]
COL_GROUPS = [[row * SIDE + col for row in range(SIDE)] for col in range(SIDE)]


def dot_nt(left, right):
    return lax.dot_general(left, right, (((1,), (1,)), ((), ())), preferred_element_type=F32)


def dot_nn(left, right):
    return lax.dot_general(left, right, (((1,), (0,)), ((), ())), preferred_element_type=F32)


def whole(count):
    return [pl.BlockSpec(memory_space=pltpu.VMEM)] * count


def chunk(index, size):
    return pl.ds(pl.multiple_of(lax.rem(index + SIDE, SIDE) * size, size), size)


def cut(row, returning, weight):
    stripe, width = returning.shape
    quarter = width // SIDE

    def body(row_ref, returning_ref, weight_ref, *outs):
        for j, out_ref in enumerate(outs):
            here = chunk(row_ref[0] - j, quarter)
            out_ref[:stripe, :] = returning_ref[:, here]
            out_ref[stripe:, :] = weight_ref[here, :].T

    return pl.pallas_call(
        body,
        in_specs=[pl.BlockSpec(memory_space=pltpu.SMEM)] + whole(2),
        out_specs=whole(SIDE),
        out_shape=[jax.ShapeDtypeStruct((2 * stripe, quarter), weight.dtype)] * SIDE,
        cost_estimate=pl.CostEstimate(
            flops=0, bytes_accessed=8 * stripe * width, transcendentals=0
        ),
    )(row[None], returning, weight)


def after(value, *others):
    return lax.optimization_barrier((value,) + others)[0]


def left_kernel(block_ref, factor_ref, x_ref, out_ref):
    out_ref[...] = dot_nt(factor_ref[...], x_ref[...]).astype(out_ref.dtype)


def left_product(block_here, factor, x):
    size = factor.shape[0]
    tokens = x.shape[0]
    return pl.pallas_call(
        left_kernel,
        grid_spec=pltpu.PrefetchScalarGridSpec(
            num_scalar_prefetch=1,
            grid=(1,),
            in_specs=[
                pl.BlockSpec((size, size), lambda i, block: (0, 0)),
                pl.BlockSpec((tokens, size), lambda i, block: (0, block[0])),
            ],
            out_specs=pl.BlockSpec((size, tokens), lambda i, block: (0, 0)),
        ),
        out_shape=jax.ShapeDtypeStruct((size, tokens), BF),
        cost_estimate=pl.CostEstimate(
            flops=2 * size * size * tokens,
            bytes_accessed=2 * size * (size + 2 * tokens),
            transcendentals=0,
        ),
    )(block_here, factor, x)


def spread_kernel(slots_ref, *refs):
    lefts, right_ref, out_ref = refs[:SIDE], refs[SIDE], refs[SIDE + 1]
    size = lefts[0].shape[0]
    for i, left_ref in enumerate(lefts):
        product = dot_nn(left_ref[...], right_ref[...])
        out_ref[i * size : (i + 1) * size, :] = product.astype(out_ref.dtype)


def spread(slots, left, right, height, width):
    depth = left.shape[1]
    place = right.shape[1] // width - 1
    block_count = slots.shape[0]
    streams = [
        pl.BlockSpec(
            (height // 2, depth), lambda b, slots, i=i: (slots[2 * b + i // 2] * 2 + i % 2, 0)
        )
        for i in range(SIDE)
    ]
    return pl.pallas_call(
        spread_kernel,
        grid_spec=pltpu.PrefetchScalarGridSpec(
            num_scalar_prefetch=1,
            grid=(block_count // 2,),
            in_specs=streams + [pl.BlockSpec((depth, width), lambda b, slots: (0, place))],
            out_specs=pl.BlockSpec((2 * height, width), lambda b, slots: (b, 0)),
        ),
        out_shape=jax.ShapeDtypeStruct((block_count * height, width), BF),
        cost_estimate=pl.CostEstimate(
            flops=2 * block_count * height * depth * width,
            bytes_accessed=2 * block_count * height * (depth + width),
            transcendentals=0,
        ),
    )(slots, *[left] * SIDE, right)


def join(own, ahead, far, behind):
    size, width = own.shape
    joined = jnp.zeros((SIDE * size, width), own.dtype)
    starts = (0, size, 3 * size, 2 * size, 2 * size + size // 2)
    for part, start in zip((own, ahead, behind) + tuple(far), starts):
        joined = lax.dynamic_update_slice(joined, part, (start, 0))
    return joined


def on_device(
    top_cotangent, inputs, proj_weight, return_weight, owners, input_inverses, output_inverses
):
    section_count = lax.axis_size("section")
    section_here = lax.axis_index("section")
    kfac_here = lax.axis_index("kfac")
    row, col = kfac_here // SIDE, kfac_here % SIDE
    core, plane = section_here % 2, section_here // 2
    odd_here = core == 1
    micro, per_micro, shard_width = top_cotangent.shape
    tokens = micro * per_micro
    group_tokens = tokens // SIDE
    x = inputs[0].reshape(tokens, -1)
    weight = proj_weight[0]
    width, stripe = weight.shape
    quarter = width // SIDE
    pair = SIDE // 2
    block_width = input_inverses.shape[2]
    block_count = width // block_width

    top = exchange(top_cotangent.reshape(SIDE, group_tokens, shard_width), ROW_GROUPS)

    slopes = silu_slope(dot_nn(x, weight)).astype(BF).reshape(1, SIDE, group_tokens, stripe)
    slopes = jnp.broadcast_to(slopes, (SIDE, SIDE, group_tokens, stripe))
    slopes = lax.all_to_all(slopes.reshape(SIDE * SIDE, group_tokens, stripe), "kfac", 0, 0)

    def odd_even(kept, received):
        return jnp.where(odd_here, kept, received), jnp.where(odd_here, received, kept)

    def in_ring_order(by_col):
        twice = jnp.concatenate([by_col, by_col], axis=1)
        return lax.dynamic_slice_in_dim(twice, col, SIDE, 1)

    def chain_factors(slopes):
        slopes = slopes.reshape(SIDE, SIDE, group_tokens, stripe)
        kept = lax.dynamic_slice_in_dim(slopes, pair * core, pair, 0)
        sent = lax.dynamic_slice_in_dim(slopes, pair * (1 - core), pair, 0)
        return [
            jnp.transpose(in_ring_order(part), (2, 1, 0, 3)).reshape(group_tokens, -1)
            for part in odd_even(kept, swap_cores(sent))
        ]

    pieces = cut(row, return_weight[0], weight)
    picks = [lax.rem(place - row + SIDE, SIDE) for place in range(SIDE)]

    def exchange_rows(core_now, first, last, *held):
        own = [after(piece, *held)[first:last] for piece in pieces]
        return own[:1] + [from_row(own[j], j, core_now) for j in range(1, SIDE)]

    def core_groups(rows, core_now, *gate):
        rows = [after(rows[0], *gate)] + rows[1:]
        groups = [
            jnp.concatenate([lax.select_n(p, *rows) for p in picks[i : i + pair]])
            for i in range(0, SIDE, pair)
        ]
        return groups[core_now], to_other_core(groups[1 - core_now], core_now)

    half = stripe
    odd = exchange_rows(1, 0, 2 * stripe)
    kept, received = core_groups([part[:stripe] for part in odd], 1, top, slopes)
    block = jnp.where(core == 1, kept, received)
    ahead, behind = from_col(block, 1), from_col(block, SIDE - 1)
    kept, received = core_groups([part[stripe:] for part in odd], 1, block)
    even = exchange_rows(0, 0, 2 * stripe, *odd[1:])
    before = even[1:]
    sent = []
    gathered = []
    for core_now in (1, 0, 0, None):
        back_half = (ahead[:half], behind[half:])
        last, near = block, (ahead, behind)
        if core_now is None:
            far = (from_col(back_half[0], 1), from_col(back_half[1], SIDE - 1))
        else:
            block = jnp.where(core == core_now, after(kept, ahead, behind, *before), received)
            sent.append([jnp.concatenate([part, block]) for part in back_half])
            ahead, behind = from_col(sent[-1][0], 1), from_col(sent[-1][1], SIDE - 1)
            before = []
            if len(sent) == 1:
                before = factors = chain_factors(after(slopes, *sent[0]))
            far = (ahead[:half], behind[:half])
            ahead, behind = ahead[half:], behind[half:]
            if len(gathered) < 2:
                kind = len(gathered) * stripe
                rows = [part[kind : kind + stripe] for part in even]
                kept, received = core_groups(rows, 0, block)
        gathered.append((last, near, far))
    back_odd, proj_odd, back_even, proj_even = [
        join(last, near[0], [after(part, *following) for part in far], near[1])
        for (last, near, far), following in zip(gathered, sent[1:] + [(), ()])
    ]
    chain_weights = ((back_odd, proj_odd), (back_even, proj_even))

    top = top.reshape(SIDE, group_tokens, shard_width)
    shard = jnp.concatenate([top[i] for i in range(SIDE)], axis=1)

    group_here = row // pair
    out_rows = lax.dynamic_slice(
        output_inverses[0],
        (group_here, 0, row % pair * SIDE * stripe),
        (1, block_width, SIDE * stripe),
    ).reshape(pair, SIDE, stripe, SIDE * stripe)
    out_rows = jnp.swapaxes(in_ring_order(out_rows), 0, 1).reshape(block_width, SIDE * stripe)

    targets = owners[0] + slot_numbers(owners[0])
    mine = targets == kfac_here
    block_here = jnp.sum(jnp.where(mine, jnp.arange(block_count, dtype=jnp.int32), 0))
    left_here = left_product(after(block_here[None], *sent[0]), input_inverses[0, 0], x)

    saved = None
    for visit in range(section_count // 2):
        new = []
        for factor, (back_now, proj_now) in zip(factors, chain_weights):
            if visit == 0:
                shard = after(shard, left_here) if new else after(shard, *sent[1])
            back = sum_rows(dot_nt(shard, back_now).astype(BF))
            slope = (back * factor).astype(BF)
            if visit == 0 and not new:
                slope = after(slope, *sent[2])
            own = dot_nn(slope, proj_now)
            summed = shard.astype(F32) + own + swap_cores(own.astype(BF)).astype(F32)
            shard = summed.astype(BF)
            new += [slope, shard]
        active = plane == section_count // 2 - 1 - visit
        saved = new if saved is None else [jnp.where(active, n, o) for n, o in zip(new, saved)]
        if visit == 0:
            left_all = lax.all_gather(after(left_here, shard), "kfac", axis=0, tiled=True)
        if visit < section_count // 2 - 1:
            shard = pass_down(shard)

    slope_odd, shard_odd, slope_even, shard_even = saved
    slope_mine = jnp.where(odd_here, slope_odd, slope_even)
    slope_other = swap_cores(jnp.where(odd_here, slope_even, slope_odd))
    slope_group = jnp.where(core == group_here, slope_mine, slope_other)
    right = dot_nn(slope_group, out_rows).astype(BF).reshape(group_tokens, SIDE, stripe)
    output = jnp.where(odd_here, shard_odd, shard_even).reshape(group_tokens, SIDE, shard_width)
    both = jnp.swapaxes(jnp.concatenate([output, right], axis=2), 0, 1)
    both = exchange(both, ROW_GROUPS).reshape(tokens, shard_width + stripe)
    outputs = both[:, :shard_width]
    result = spread(targets, left_all, both, block_width, stripe)
    return outputs.reshape(1, micro, per_micro, shard_width), result[None]


def solution(mesh):
    return jax.shard_map(
        on_device,
        mesh=mesh,
        in_specs=(
            P(None, None, "kfac"),
            P("section", None, None, None),
            P("section", None, "kfac"),
            P("section", "kfac", None),
            P("section", None),
            P("section", "kfac", None, None),
            P("section", None, None, None),
        ),
        out_specs=(P("section", None, None, "kfac"), P("section", None, "kfac")),
        check_vma=False,
    )
```

```python
import jax
import jax.numpy as jnp
from jax import lax
from jax.experimental import pallas as pl
from jax.experimental.pallas import tpu as pltpu
from jax.sharding import PartitionSpec as P

BF = jnp.bfloat16
F32 = jnp.float32
SIDE = 4


def silu_slope(values):
    sigmoid = jax.nn.sigmoid(values)
    return sigmoid * (1.0 + values * (1.0 - sigmoid))


def slot_numbers(owner_row):
    blocks = owner_row.shape[0]
    earlier = jnp.arange(blocks)[None, :] < jnp.arange(blocks)[:, None]
    shared = owner_row[None, :] == owner_row[:, None]
    return jnp.sum(jnp.logical_and(earlier, shared).astype(jnp.int32), axis=1)


def permute_grid(block, source):
    route = []
    for row in range(SIDE):
        for col in range(SIDE):
            from_row, from_col = source(row, col)
            route.append((from_row * SIDE + from_col, row * SIDE + col))
    return lax.ppermute(block, "kfac", route)


def from_col(block, distance):
    return permute_grid(block, lambda row, col: (row, (col + distance) % SIDE))


def from_row(block, distance, core):
    size = SIDE * SIDE
    route = []
    for section in range(core, lax.axis_size("section"), 2):
        for row in range(SIDE):
            for col in range(SIDE):
                source = (row + distance) % SIDE * SIDE + col
                route.append((section * size + source, section * size + row * SIDE + col))
    return lax.ppermute(block, ("section", "kfac"), route)


def to_other_core(block, core):
    sections = range(core, lax.axis_size("section"), 2)
    return lax.ppermute(block, "section", [(i, i ^ 1) for i in sections])


def swap_cores(block):
    sections = lax.axis_size("section")
    return lax.ppermute(block, "section", [(i, i ^ 1) for i in range(sections)])


def pass_down(block):
    sections = lax.axis_size("section")
    return lax.ppermute(block, "section", [(i, i - 2) for i in range(2, sections)])


def sum_rows(block):
    near = permute_grid(block, lambda row, col: (row ^ 1, col))
    half = (block.astype(F32) + near.astype(F32)).astype(BF)
    far = permute_grid(half, lambda row, col: (SIDE - 1 - row, col))
    return half.astype(F32) + far.astype(F32)


def exchange(pieces, groups):
    return lax.all_to_all(pieces, "kfac", 0, 0, axis_index_groups=groups)


ROW_GROUPS = [[row * SIDE + col for col in range(SIDE)] for row in range(SIDE)]
COL_GROUPS = [[row * SIDE + col for row in range(SIDE)] for col in range(SIDE)]


def dot_nt(left, right):
    return lax.dot_general(left, right, (((1,), (1,)), ((), ())), preferred_element_type=F32)


def dot_nn(left, right):
    return lax.dot_general(left, right, (((1,), (0,)), ((), ())), preferred_element_type=F32)


def whole(count):
    return [pl.BlockSpec(memory_space=pltpu.VMEM)] * count


def chunk(index, size):
    return pl.ds(pl.multiple_of(lax.rem(index + SIDE, SIDE) * size, size), size)


def cut(row, returning, weight):
    stripe, width = returning.shape
    quarter = width // SIDE

    def body(row_ref, returning_ref, weight_ref, *outs):
        for j, out_ref in enumerate(outs):
            here = chunk(row_ref[0] - j, quarter)
            out_ref[:stripe, :] = returning_ref[:, here]
            out_ref[stripe:, :] = weight_ref[here, :].T

    return pl.pallas_call(
        body,
        in_specs=[pl.BlockSpec(memory_space=pltpu.SMEM)] + whole(2),
        out_specs=whole(SIDE),
        out_shape=[jax.ShapeDtypeStruct((2 * stripe, quarter), weight.dtype)] * SIDE,
        cost_estimate=pl.CostEstimate(
            flops=0, bytes_accessed=8 * stripe * width, transcendentals=0
        ),
    )(row[None], returning, weight)


def after(value, *others):
    return lax.optimization_barrier((value,) + others)[0]


def left_kernel(block_ref, factor_ref, x_ref, out_ref):
    out_ref[...] = dot_nt(factor_ref[...], x_ref[...]).astype(out_ref.dtype)


def left_product(block_here, factor, x):
    size = factor.shape[0]
    tokens = x.shape[0]
    return pl.pallas_call(
        left_kernel,
        grid_spec=pltpu.PrefetchScalarGridSpec(
            num_scalar_prefetch=1,
            grid=(1,),
            in_specs=[
                pl.BlockSpec((size, size), lambda i, block: (0, 0)),
                pl.BlockSpec((tokens, size), lambda i, block: (0, block[0])),
            ],
            out_specs=pl.BlockSpec((size, tokens), lambda i, block: (0, 0)),
        ),
        out_shape=jax.ShapeDtypeStruct((size, tokens), BF),
        cost_estimate=pl.CostEstimate(
            flops=2 * size * size * tokens,
            bytes_accessed=2 * size * (size + 2 * tokens),
            transcendentals=0,
        ),
    )(block_here, factor, x)


def spread_kernel(slots_ref, *refs):
    lefts, right_ref, out_ref = refs[:SIDE], refs[SIDE], refs[SIDE + 1]
    size = lefts[0].shape[0]
    for i, left_ref in enumerate(lefts):
        product = dot_nn(left_ref[...], right_ref[...])
        out_ref[i * size : (i + 1) * size, :] = product.astype(out_ref.dtype)


def spread(slots, left, right, height, width):
    depth = left.shape[1]
    place = right.shape[1] // width - 1
    block_count = slots.shape[0]
    streams = [
        pl.BlockSpec(
            (height // 2, depth), lambda b, slots, i=i: (slots[2 * b + i // 2] * 2 + i % 2, 0)
        )
        for i in range(SIDE)
    ]
    return pl.pallas_call(
        spread_kernel,
        grid_spec=pltpu.PrefetchScalarGridSpec(
            num_scalar_prefetch=1,
            grid=(block_count // 2,),
            in_specs=streams + [pl.BlockSpec((depth, width), lambda b, slots: (0, place))],
            out_specs=pl.BlockSpec((2 * height, width), lambda b, slots: (b, 0)),
        ),
        out_shape=jax.ShapeDtypeStruct((block_count * height, width), BF),
        cost_estimate=pl.CostEstimate(
            flops=2 * block_count * height * depth * width,
            bytes_accessed=2 * block_count * height * (depth + width),
            transcendentals=0,
        ),
    )(slots, *[left] * SIDE, right)


def join(own, ahead, far, behind):
    size, width = own.shape
    joined = jnp.zeros((SIDE * size, width), own.dtype)
    starts = (0, size, 3 * size, 2 * size, 2 * size + size // 2)
    for part, start in zip((own, ahead, behind) + tuple(far), starts):
        joined = lax.dynamic_update_slice(joined, part, (start, 0))
    return joined


def on_device(
    top_cotangent, inputs, proj_weight, return_weight, owners, input_inverses, output_inverses
):
    section_count = lax.axis_size("section")
    section_here = lax.axis_index("section")
    kfac_here = lax.axis_index("kfac")
    row, col = kfac_here // SIDE, kfac_here % SIDE
    core, plane = section_here % 2, section_here // 2
    odd_here = core == 1
    micro, per_micro, shard_width = top_cotangent.shape
    tokens = micro * per_micro
    group_tokens = tokens // SIDE
    x = inputs[0].reshape(tokens, -1)
    weight = proj_weight[0]
    width, stripe = weight.shape
    quarter = width // SIDE
    pair = SIDE // 2
    block_width = input_inverses.shape[2]
    block_count = width // block_width

    top = exchange(top_cotangent.reshape(SIDE, group_tokens, shard_width), ROW_GROUPS)

    slopes = silu_slope(dot_nn(x, weight)).astype(BF).reshape(1, SIDE, group_tokens, stripe)
    slopes = jnp.broadcast_to(slopes, (SIDE, SIDE, group_tokens, stripe))
    slopes = lax.all_to_all(slopes.reshape(SIDE * SIDE, group_tokens, stripe), "kfac", 0, 0)

    def odd_even(kept, received):
        return jnp.where(odd_here, kept, received), jnp.where(odd_here, received, kept)

    def in_ring_order(by_col):
        twice = jnp.concatenate([by_col, by_col], axis=1)
        return lax.dynamic_slice_in_dim(twice, col, SIDE, 1)

    def chain_factors(slopes):
        slopes = slopes.reshape(SIDE, SIDE, group_tokens, stripe)
        kept = lax.dynamic_slice_in_dim(slopes, pair * core, pair, 0)
        sent = lax.dynamic_slice_in_dim(slopes, pair * (1 - core), pair, 0)
        return [
            jnp.transpose(in_ring_order(part), (2, 1, 0, 3)).reshape(group_tokens, -1)
            for part in odd_even(kept, swap_cores(sent))
        ]

    pieces = cut(row, return_weight[0], weight)
    picks = [lax.rem(place - row + SIDE, SIDE) for place in range(SIDE)]

    def exchange_rows(core_now, first, last, *held):
        own = [after(piece, *held)[first:last] for piece in pieces]
        return own[:1] + [from_row(own[j], j, core_now) for j in range(1, SIDE)]

    def core_groups(rows, core_now, *gate):
        rows = [after(rows[0], *gate)] + rows[1:]
        groups = [
            jnp.concatenate([lax.select_n(p, *rows) for p in picks[i : i + pair]])
            for i in range(0, SIDE, pair)
        ]
        return groups[core_now], to_other_core(groups[1 - core_now], core_now)

    half = stripe
    odd = exchange_rows(1, 0, 2 * stripe)
    kept, received = core_groups([part[:stripe] for part in odd], 1, top, slopes)
    block = jnp.where(core == 1, kept, received)
    ahead, behind = from_col(block, 1), from_col(block, SIDE - 1)
    kept, received = core_groups([part[stripe:] for part in odd], 1, block)
    even = exchange_rows(0, 0, 2 * stripe, *odd[1:])
    before = even[1:]
    sent = []
    gathered = []
    for core_now in (1, 0, 0, None):
        back_half = (ahead[:half], behind[half:])
        last, near = block, (ahead, behind)
        if core_now is None:
            far = (from_col(back_half[0], 1), from_col(back_half[1], SIDE - 1))
        else:
            block = jnp.where(core == core_now, after(kept, ahead, behind, *before), received)
            sent.append([jnp.concatenate([part, block]) for part in back_half])
            ahead, behind = from_col(sent[-1][0], 1), from_col(sent[-1][1], SIDE - 1)
            before = []
            if len(sent) == 1:
                before = factors = chain_factors(after(slopes, *sent[0]))
            far = (ahead[:half], behind[:half])
            ahead, behind = ahead[half:], behind[half:]
            if len(gathered) < 2:
                kind = len(gathered) * stripe
                rows = [part[kind : kind + stripe] for part in even]
                kept, received = core_groups(rows, 0, *sent[-1])
        gathered.append((last, near, far))
    back_odd, proj_odd, back_even, proj_even = [
        join(last, near[0], [after(part, *following) for part in far], near[1])
        for (last, near, far), following in zip(gathered, sent[1:] + [(), ()])
    ]
    chain_weights = ((back_odd, proj_odd), (back_even, proj_even))

    top = top.reshape(SIDE, group_tokens, shard_width)
    shard = jnp.concatenate([top[i] for i in range(SIDE)], axis=1)

    group_here = row // pair
    out_rows = lax.dynamic_slice(
        output_inverses[0],
        (group_here, 0, row % pair * SIDE * stripe),
        (1, block_width, SIDE * stripe),
    ).reshape(pair, SIDE, stripe, SIDE * stripe)
    out_rows = jnp.swapaxes(in_ring_order(out_rows), 0, 1).reshape(block_width, SIDE * stripe)

    targets = owners[0] + slot_numbers(owners[0])
    mine = targets == kfac_here
    block_here = jnp.sum(jnp.where(mine, jnp.arange(block_count, dtype=jnp.int32), 0))
    left_here = left_product(after(block_here[None], *sent[0]), input_inverses[0, 0], x)

    saved = None
    for visit in range(section_count // 2):
        new = []
        for factor, (back_now, proj_now) in zip(factors, chain_weights):
            if visit == 0:
                shard = after(shard, left_here) if new else after(shard, *sent[1])
            back = sum_rows(dot_nt(shard, back_now).astype(BF))
            slope = (back * factor).astype(BF)
            if visit == 0 and not new:
                slope = after(slope, *sent[2])
            own = dot_nn(slope, proj_now)
            summed = shard.astype(F32) + own + swap_cores(own.astype(BF)).astype(F32)
            shard = summed.astype(BF)
            new += [slope, shard]
        active = plane == section_count // 2 - 1 - visit
        saved = new if saved is None else [jnp.where(active, n, o) for n, o in zip(new, saved)]
        if visit == 0:
            left_all = lax.all_gather(after(left_here, shard), "kfac", axis=0, tiled=True)
        if visit < section_count // 2 - 1:
            shard = pass_down(shard)

    slope_odd, shard_odd, slope_even, shard_even = saved
    slope_mine = jnp.where(odd_here, slope_odd, slope_even)
    slope_other = swap_cores(jnp.where(odd_here, slope_even, slope_odd))
    slope_group = jnp.where(core == group_here, slope_mine, slope_other)
    right = dot_nn(slope_group, out_rows).astype(BF).reshape(group_tokens, SIDE, stripe)
    output = jnp.where(odd_here, shard_odd, shard_even).reshape(group_tokens, SIDE, shard_width)
    both = jnp.swapaxes(jnp.concatenate([output, right], axis=2), 0, 1)
    both = exchange(both, ROW_GROUPS).reshape(tokens, shard_width + stripe)
    outputs = both[:, :shard_width]
    result = spread(targets, left_all, both, block_width, stripe)
    return outputs.reshape(1, micro, per_micro, shard_width), result[None]


def solution(mesh):
    return jax.shard_map(
        on_device,
        mesh=mesh,
        in_specs=(
            P(None, None, "kfac"),
            P("section", None, None, None),
            P("section", None, "kfac"),
            P("section", "kfac", None),
            P("section", None),
            P("section", "kfac", None, None),
            P("section", None, None, None),
        ),
        out_specs=(P("section", None, None, "kfac"), P("section", None, "kfac")),
        check_vma=False,
    )
```
